32 devices in a mesh: groups: 2 (over x), cells: 16 (over z, y, core).
Axes of the slice: x: 2, y: 2, z: 4, core: 2. Of those that a mesh axis runs over, the one named last changes fastest.
Arguments:
- footprints: bfloat16 [256, 128, 128], P(('groups', 'cells')), parts along dimension 0, may hold values from -0.1875 to 0.1875
- tile_rows: int32 [256], P(('groups', 'cells')), parts along dimension 0, may hold values from 0 to 7
- tile_cols: int32 [256], P(('groups', 'cells')), parts along dimension 0, may hold values from 0 to 15
- tile_counts: int32 [32], P(('groups', 'cells')), parts along dimension 0, may hold values from 1 to 8, as said below
- coords: float32 [2, 8192], P(None, ('groups', 'cells')), parts along dimension 1, may hold values from 0 to 3
- obs_error: float32 [2048], P(('groups', 'cells')), parts along dimension 0, may hold values from 0.5 to 2
Outputs:
- covariance: float32 [2048, 1024], P(('groups', 'cells')), parts along dimension 0
The draws below stay inside these ranges and needn't reach their ends.
There are 2 independent parts, one for each index of `groups`. The reference program is written for one: setup_inputs(seed, part) draws one part's arguments, and reference() takes and returns one part's arrays. A program takes and returns all parts, laid end to end along the dimension named above; each array names one. Nothing has to cross between parts.
Inputs may be any that keep to these rules, and one draw needn't show every extreme that they name: The first tile_counts[c] slots of device c are live, the rest are ignored; in every draw some device has all 8 slots live.
All inputs are finite; a program needn't handle non-finite values.
Results may differ from the reference program's by a relative error of at most 0.0038.
Values may be sent and summed in bfloat16 or wider, within the bound.
A program may use at most 64 MiB of HBM per device.

```python
import math
import jax
import jax.numpy as jnp
from jax import lax

TILE = 128
WEEKS = 8
TILE_CAP = 8
OBS = 1024
CELL_DEV = 256
NCELLS = 4096
SLOTS = 128
N_CELLS = 16


def draw_tile_counts(key, part):
    key = jax.random.fold_in(key, 11)
    first_key, second_key = jax.random.split(key)
    counts = jax.random.randint(first_key, (N_CELLS,), 1, TILE_CAP + 1)
    filled = jax.random.randint(second_key, (), 0, N_CELLS)
    return jnp.where(jnp.arange(N_CELLS) == filled, TILE_CAP, counts).astype(jnp.int32)


def set_ends(array, stream_key, smallest, high):
    dims = array.shape
    spot = [jax.random.randint(jax.random.fold_in(stream_key, axis), (), 0, dims[axis]) for axis in range(len(dims))]
    array = array.at[tuple(spot)].set(smallest)
    longest = dims.index(max(dims))
    spot[longest] = (spot[longest] + 1) % dims[longest]
    return array.at[tuple(spot)].set(high)


def steps_of(own_key, dims, pieces, least, largest):
    loudness = 1.0
    for position, shards_of in pieces:
        heights = jax.random.uniform(jax.random.fold_in(jax.random.fold_in(own_key, 6), position), (shards_of,), jnp.float32, least / len(pieces), largest / len(pieces))
        loudness = loudness * jnp.repeat(jnp.exp(heights), dims[position] // shards_of).reshape((-1,) + (1,) * (len(dims) - 1 - position))
    return loudness


def noise(key, extent, scale, most, pieces=(), kind=jnp.bfloat16):
    entries = jax.random.normal(key, extent, jnp.float32) * scale
    if len(pieces) > 0:
        entries = steps_of(key, extent, pieces, -0.22, 0.18) * entries
    return jnp.clip(entries, min=-most, max=most).astype(kind)


def setup_inputs(seed: int = 0, part: int = 0) -> dict:
    seeds = jax.random.split(jax.random.key(seed), 7)
    part_keys = jax.random.split(jax.random.fold_in(seeds[6], part), 7)
    return {
        "footprints": noise(part_keys[0], (SLOTS, TILE, TILE), (TILE * N_CELLS * (TILE_CAP + 1) // (2 * (OBS // TILE))) ** -0.5, 0.1875, ((0, 16),)),
        "tile_rows": set_ends(jax.random.randint(part_keys[1], (SLOTS,), 0, OBS // TILE), jax.random.fold_in(part_keys[1], 1), 0, (OBS // TILE) - 1).astype(jnp.int32),
        "tile_cols": set_ends(jax.random.randint(part_keys[2], (SLOTS,), 0, WEEKS * CELL_DEV // TILE), jax.random.fold_in(part_keys[2], 1), 0, (WEEKS * CELL_DEV // TILE) - 1).astype(jnp.int32),
        "tile_counts": draw_tile_counts(jax.random.fold_in(jax.random.fold_in(seeds[6], part), 71), part),
        "coords": jnp.clip(3.0 * jax.random.uniform(part_keys[4], (2, NCELLS), jnp.float32) ** steps_of(part_keys[4], (2, NCELLS), ((1, 16),), -0.2, 0.2), 0.0, 3.0),
        "obs_error": jnp.clip(jnp.exp(math.log(2.0) - 1.3862944 * jax.random.uniform(part_keys[5], (OBS,), jnp.float32) ** steps_of(part_keys[5], (OBS,), ((0, 16),), -0.2, 0.2)), 0.5, 2.0),
    }


SPACE_RANGE = 1.0
TIME_RANGE = 3.0

def space_block(home_pos, visitor_pos):
    east_gap = home_pos[0][:, None] - visitor_pos[0][None, :]
    north_gap = home_pos[1][:, None] - visitor_pos[1][None, :]
    return jnp.exp(-jnp.sqrt(east_gap * east_gap + north_gap * north_gap) / SPACE_RANGE).astype(jnp.bfloat16)

def absorb(accumulator, tile_stack, row_index, col_index, live_count, covar):
    slot_count, tile_edge = (tile_stack.shape[0], tile_stack.shape[1])
    weeks, cell_count, obs_count = accumulator.shape
    per_week = cell_count // tile_edge
    week_index = (col_index // per_week).astype(jnp.int32)
    cell_block = (col_index % per_week).astype(jnp.int32)
    strips = jnp.take(covar.reshape(cell_count, per_week, tile_edge), cell_block, axis=1)
    products = jnp.einsum('isj,smj->sim', strips, tile_stack, preferred_element_type=jnp.float32)
    live = jnp.arange(slot_count, dtype=jnp.int32) < live_count
    products = jnp.where(live[:, None, None], products, jnp.zeros_like(products))
    blocked = accumulator.reshape(weeks, cell_count, obs_count // tile_edge, tile_edge)
    blocked = blocked.at[week_index, :, row_index.astype(jnp.int32), :].add(products)
    return blocked.reshape(weeks, cell_count, obs_count)

def own_rows(running, weighted, tile_stack, row_index, col_index, live_count):
    slot_count, tile_edge = (tile_stack.shape[0], tile_stack.shape[1])
    weeks, cell_count, obs_count = weighted.shape
    per_week = cell_count // tile_edge
    week_index = (col_index // per_week).astype(jnp.int32)
    cell_block = (col_index % per_week).astype(jnp.int32)
    strips = weighted.reshape(weeks, per_week, tile_edge, obs_count)[week_index, cell_block]
    partial_value = jnp.einsum('smj,sjn->smn', tile_stack, strips, preferred_element_type=jnp.float32)
    live = jnp.arange(slot_count, dtype=jnp.int32) < live_count
    partial_value = jnp.where(live[:, None, None], partial_value, jnp.zeros_like(partial_value))
    blocked = running.reshape(running.shape[0] // tile_edge, tile_edge, running.shape[1])
    blocked = blocked.at[row_index.astype(jnp.int32)].add(partial_value)
    return blocked.reshape(running.shape)

def time_matrix():
    week_axis = jnp.arange(WEEKS).astype(jnp.float32)
    return jnp.exp(-jnp.abs(week_axis[:, None] - week_axis[None, :]) / TIME_RANGE)

def reference(footprints, tile_rows, tile_cols, tile_counts, coords, obs_error):
    tile_stack = footprints.reshape(N_CELLS, TILE_CAP, TILE, TILE)
    row_table = tile_rows.reshape(N_CELLS, TILE_CAP)
    col_table = tile_cols.reshape(N_CELLS, TILE_CAP)
    positions = coords.reshape(2, N_CELLS, CELL_DEV).transpose(1, 0, 2)
    time_cov = time_matrix()

    def owner(running, owner_index):
        home_pos = positions[owner_index]

        def visit_one(accumulator, visitor):
            covar = space_block(home_pos, positions[visitor])
            accumulator = absorb(accumulator, tile_stack[visitor], row_table[visitor], col_table[visitor], tile_counts[visitor], covar)
            return (accumulator, None)
        spread, _ = lax.scan(visit_one, jnp.zeros((WEEKS, CELL_DEV, OBS), jnp.float32), jnp.arange(N_CELLS))
        weighted = jnp.einsum('wv,vim->wim', time_cov, spread, precision=lax.Precision.HIGHEST).astype(jnp.bfloat16)
        running = own_rows(running, weighted, tile_stack[owner_index], row_table[owner_index], col_table[owner_index], tile_counts[owner_index])
        return (running, None)
    running, _ = lax.scan(owner, jnp.zeros((OBS, OBS), jnp.float32), jnp.arange(N_CELLS))
    return running + jnp.diag(obs_error)
```

```python
import functools

import jax
import jax.numpy as jnp
from jax import lax
from jax.experimental import pallas as pl
from jax.experimental.pallas import tpu as pltpu
from jax.sharding import PartitionSpec as P

WEEKS = 8
OBS = 1024
TILE = 128
SPACE_RANGE = 1.0
TIME_RANGE = 3.0
CHUNKS = 2
VMEM_BYTES = 56 * 1024 * 1024


def place(lines):
    me = lax.axis_index("cells")
    chip = me // 2
    return me, me % 2, chip, chip % lines, chip // lines


def remote(src, dst, send, recv, target):
    return pltpu.make_async_remote_copy(
        src_ref=src,
        dst_ref=dst,
        send_sem=send,
        recv_sem=recv,
        device_id={"cells": target},
        device_id_type=pl.DeviceIdType.MESH,
    )


def signal(sem, target):
    pl.semaphore_signal(
        sem, inc=1, device_id={"cells": target}, device_id_type=pl.DeviceIdType.MESH
    )


def gather_kernel(
    chips, lines, own, packet, tiles, home_tiles, covar, meta,
    packets, home_pos, pkt_send, pkt_recv, sib_send, sib_recv, hop_send, hop_recv,
):
    depth = chips // lines
    me, core, chip, y, z = place(lines)
    sibling = me + 1 - 2 * core
    slots = own.shape[0]
    part = slots // CHUNKS
    cells = home_pos.shape[1] // 2
    per_dev = cells // TILE

    barrier = pltpu.get_barrier_semaphore()
    for k in range(1, chips):
        signal(barrier, lax.rem(chip + k, chips) * 2 + core)
    signal(barrier, sibling)
    pl.semaphore_wait(barrier, chips)

    pkt_copies = [remote(packet, packets.at[chips], pkt_send.at[0], pkt_recv.at[0], sibling)]
    for k in range(1, chips):
        pkt_copies.append(
            remote(packet, packets.at[chip], pkt_send.at[k], pkt_recv.at[k],
                   lax.rem(chip + k, chips) * 2 + core)
        )
    for copy in pkt_copies:
        copy.start()

    def block(q, ch):
        return tiles.at[pl.ds(q * slots + ch * part, part)]

    sends = []

    def send(cond, kind, step, q, ch, target, first):
        source = own.at[pl.ds(ch * part, part)] if first else block(q, ch)
        copy = remote(source, block(q, ch), hop_send.at[kind, step, ch],
                      hop_recv.at[q * CHUNKS + ch], target)
        sends.append((cond, copy))
        if cond is None:
            copy.start()
        else:
            pl.when(cond)(copy.start)

    def arrive(q, ch):
        remote(block(q, ch), block(q, ch), hop_send.at[0, 0, 0],
               hop_recv.at[q * CHUNKS + ch], sibling).wait_recv()

    above = me + 2 * lines
    below = me - 2 * lines
    across = me + 2 - 4 * y
    for ch in range(CHUNKS):
        send(z < depth - 1, 0, 0, chip, ch, above, True)
        send(z > 0, 1, 0, chip, ch, below, True)
        if lines == 2:
            send(None, 2, 0, chip, ch, across, True)
    sib_copy = remote(own, home_tiles.at[pl.ds(core * slots, slots)], sib_send, sib_recv, sibling)
    sib_copy.start()
    tiles[pl.ds(chip * slots, slots)] = own[...]
    home_tiles[pl.ds(core * slots, slots)] = own[...]
    packets[chip] = packet[...]

    for copy in pkt_copies:
        copy.wait()

    mine = packet[...]
    other = packets[chips]
    is_first = (core == 0).astype(jnp.float32)
    pair = (mine * is_first + other * (1.0 - is_first), other * is_first + mine * (1.0 - is_first))
    for q in range(chips):
        meta[q] = packets[q].astype(jnp.int32)
    for j in range(2):
        meta[chips + j] = pair[j].astype(jnp.int32)
        columns = jnp.transpose(pair[j])
        for b in range(per_dev):
            rows = pl.ds(j * cells + b * TILE, TILE)
            for axis in range(2):
                col = columns[:, axis * per_dev + b : axis * per_dev + b + 1]
                home_pos[axis, rows, :] = jnp.broadcast_to(col, (TILE, TILE))

    step_rows = 64

    @pl.loop(0, chips)
    def _(q):
        for b in range(per_dev):
            east = packets[q, b : b + 1, :]
            north = packets[q, per_dev + b : per_dev + b + 1, :]

            @pl.loop(0, home_pos.shape[1] // step_rows)
            def _(i):
                rows = pl.ds(i * step_rows, step_rows)
                dx = home_pos[0, rows, :] - east
                dy = home_pos[1, rows, :] - north
                covar[q * per_dev + b, rows, :] = jnp.exp(
                    -jnp.sqrt(dx * dx + dy * dy) / SPACE_RANGE
                ).astype(jnp.bfloat16)

    for d in range(1, depth):
        for ch in range(CHUNKS):
            def from_below(d=d, ch=ch):
                arrive((z - d) * lines + y, ch)

            def from_above(d=d, ch=ch):
                arrive((z + d) * lines + y, ch)

            q_low = (z - d) * lines + y
            q_high = (z + d) * lines + y
            pl.when(z >= d)(from_below)
            if d < depth - 1:
                send((z >= d) & (z < depth - 1), 0, d, q_low, ch, above, False)
            if lines == 2:
                send(z >= d, 2, d, q_low, ch, across, False)
            pl.when(z + d < depth)(from_above)
            if d < depth - 1:
                send((z + d < depth) & (z > 0), 1, d, q_high, ch, below, False)
            if lines == 2:
                send(z + d < depth, 3, d, q_high, ch, across, False)
    if lines == 2:
        for zz in range(depth):
            for ch in range(CHUNKS):
                arrive(zz * lines + 1 - y, ch)
    for cond, copy in sends:
        if cond is None:
            copy.wait_send()
        else:
            pl.when(cond)(copy.wait_send)
    sib_copy.wait()


def spread_kernel(chips, meta, tiles, home_tiles, covar, out, acc, weighted):
    slots = tiles.shape[0] // chips
    homes = covar.shape[1]
    cells = homes // 2
    per_dev = cells // TILE
    row_tiles = OBS // TILE

    @pl.loop(0, WEEKS * row_tiles)
    def _(i):
        acc[i] = jnp.zeros((homes, TILE), jnp.float32)

    def place_of(d, s):
        col = meta[d, 4, slots + s]
        return meta[d, 4, s], col // per_dev, col % per_dev

    @pl.loop(0, chips)
    def _(q):
        @pl.loop(0, meta[q, 4, 2 * slots])
        def _(s):
            row, week, b = place_of(q, s)
            strip = covar[q * per_dev + b]
            product = lax.dot_general(
                strip, tiles[q * slots + s], (((1,), (1,)), ((), ())),
                preferred_element_type=jnp.float32,
            )
            acc[week * row_tiles + row] += product

    decay = jnp.exp(jnp.float32(-1.0 / TIME_RANGE))
    step_rows = 16
    for r in range(row_tiles):
        @pl.loop(0, homes // step_rows)
        def _(i):
            rows = pl.ds(i * step_rows, step_rows)
            spread = [acc[w * row_tiles + r, rows, :] for w in range(WEEKS)]
            ahead = [spread[0]]
            for w in range(1, WEEKS):
                ahead.append(spread[w] + decay * ahead[-1])
            back = None
            for w in reversed(range(WEEKS)):
                total = ahead[w] if back is None else ahead[w] + back
                weighted[w, rows, r * TILE : (r + 1) * TILE] = total.astype(jnp.bfloat16)
                back = decay * (spread[w] if back is None else spread[w] + back)

    out[...] = jnp.zeros_like(out)
    for j in range(2):
        @pl.loop(0, meta[chips + j, 4, 2 * slots])
        def _(s):
            row, week, b = place_of(chips + j, s)
            slab = weighted[week, pl.ds(pl.multiple_of(j * cells + b * TILE, TILE), TILE), :]
            product = jnp.dot(
                home_tiles[j * slots + s], slab, preferred_element_type=jnp.float32
            )
            out[pl.ds(pl.multiple_of(row * TILE, TILE), TILE), :] += product


def reduce_kernel(
    chips, lines, partial, obs, out, sib, y_out, y_in, z_out, z_in,
    sib_send, sib_recv, y_send, y_recv, z_send, z_recv,
):
    depth = chips // lines
    me, core, chip, y, z = place(lines)
    sibling = me + 1 - 2 * core
    rows = out.shape[0]
    above = me + 2 * lines
    below = me - 2 * lines
    across = me + 2 - 4 * y
    up_ok = z < depth - 1
    down_ok = z > 0

    barrier = pltpu.get_barrier_semaphore()
    signal(barrier, sibling)
    if lines == 2:
        signal(barrier, across)
    pl.when(up_ok)(lambda: signal(barrier, above))
    pl.when(down_ok)(lambda: signal(barrier, below))
    pl.semaphore_wait(barrier, lines + up_ok.astype(jnp.int32) + down_ok.astype(jnp.int32))

    upper = (z >= depth // 2).astype(jnp.int32)

    def order(j):
        if j == depth - 1:
            return z
        high = depth - 1 - j
        high = high - (high <= z).astype(jnp.int32)
        low = j + (j >= z).astype(jnp.int32)
        return upper * low + (1 - upper) * high

    def slab(q, k):
        return partial.at[pl.ds(pl.multiple_of((q * 2 + k) * rows, 8), rows)]

    def sib_copy(q):
        return remote(slab(q, 1 - core), sib.at[q], sib_send.at[q], sib_recv.at[q], sibling)

    columns = list(reversed(range(lines)))
    for line in columns:
        for j in range(depth):
            sib_copy(order(j) * lines + (y + line) % lines).start()

    def chip_sum(q):
        sib_copy(q).wait_recv()
        return slab(q, core)[...] + sib[q]

    if lines == 2:
        for j in range(depth):
            c = order(j)
            y_out[c] = chip_sum(c * lines + 1 - y).astype(jnp.bfloat16)
            remote(y_out.at[c], y_in.at[c], y_send.at[c], y_recv.at[c], across).start()

    def up_copy(c):
        return remote(z_out.at[c], z_in.at[0, c], z_send.at[c], z_recv.at[0, c], above)

    def down_copy(c):
        return remote(z_out.at[c], z_in.at[1, c], z_send.at[c], z_recv.at[1, c], below)

    for j in range(depth - 1):
        c = order(j)
        total = chip_sum(c * lines + y)
        if lines == 2:
            remote(y_out.at[c], y_in.at[c], y_send.at[c], y_recv.at[c], across).wait_recv()
            total = total + y_in[c].astype(jnp.float32)
        out[...] = total

        @pl.when((c > z) & down_ok)
        def _():
            up_copy(c).wait_recv()
            out[...] += z_in[0, c].astype(jnp.float32)

        @pl.when((c < z) & up_ok)
        def _():
            down_copy(c).wait_recv()
            out[...] += z_in[1, c].astype(jnp.float32)

        z_out[c] = out[...].astype(jnp.bfloat16)

        @pl.when(c > z)
        def _():
            up_copy(c).start()

        @pl.when(c < z)
        def _():
            down_copy(c).start()

    total = chip_sum(chip)
    if lines == 2:
        remote(y_out.at[z], y_in.at[z], y_send.at[z], y_recv.at[z], across).wait_recv()
        total = total + y_in[z].astype(jnp.float32)
    shape = (rows, rows)
    eye = lax.broadcasted_iota(jnp.int32, shape, 0) == lax.broadcasted_iota(jnp.int32, shape, 1)
    errors = jnp.sum(
        jnp.where(eye, jnp.broadcast_to(obs[...], shape), 0.0), axis=1, keepdims=True
    )
    hit = lax.broadcasted_iota(jnp.int32, out.shape, 1) == (
        me * rows + lax.broadcasted_iota(jnp.int32, out.shape, 0)
    )
    out[...] = total + jnp.where(hit, jnp.broadcast_to(errors, out.shape), 0.0)

    @pl.when(down_ok)
    def _():
        up_copy(z).wait_recv()
        out[...] += z_in[0, z].astype(jnp.float32)

    @pl.when(up_ok)
    def _():
        down_copy(z).wait_recv()
        out[...] += z_in[1, z].astype(jnp.float32)

    for q in range(chips):
        sib_copy(q).wait_send()
    for c in range(depth):
        if lines == 2:
            remote(y_out.at[c], y_in.at[c], y_send.at[c], y_recv.at[c], across).wait_send()
        pl.when(c != z)(lambda c=c: up_copy(c).wait_send())


def local(footprints, tile_rows, tile_cols, tile_counts, coords, obs_error):
    count = lax.axis_size("cells")
    chips = count // 2
    lines = 2 if chips == 8 else 1
    depth = chips // lines
    slots = footprints.shape[0]
    cells = coords.shape[1]
    per_dev = cells // TILE
    rows = OBS // count
    vmem = pl.BlockSpec(memory_space=pltpu.VMEM)
    smem = pl.BlockSpec(memory_space=pltpu.SMEM)
    dma = pltpu.SemaphoreType.DMA

    places = jnp.concatenate([tile_rows, tile_cols, tile_counts]).astype(jnp.float32)
    places = jnp.pad(places, (0, TILE - places.shape[0]))
    packet = jnp.concatenate([coords.reshape(2 * per_dev, TILE), places[None, :]], axis=0)
    packet = jnp.pad(packet, ((0, 8 - packet.shape[0]), (0, 0)))

    tiles, home_tiles, covar, meta = pl.pallas_call(
        functools.partial(gather_kernel, chips, lines),
        out_shape=(
            jax.ShapeDtypeStruct((chips * slots, TILE, TILE), jnp.bfloat16),
            jax.ShapeDtypeStruct((2 * slots, TILE, TILE), jnp.bfloat16),
            jax.ShapeDtypeStruct((chips * per_dev, 2 * cells, TILE), jnp.bfloat16),
            jax.ShapeDtypeStruct((chips + 2, 8, TILE), jnp.int32),
        ),
        in_specs=[vmem] * 2,
        out_specs=(vmem,) * 4,
        scratch_shapes=[
            pltpu.VMEM((chips + 1, 8, TILE), jnp.float32),
            pltpu.VMEM((2, 2 * cells, TILE), jnp.float32),
            dma((chips,)),
            dma((chips,)),
            dma,
            dma,
            dma((4, depth, CHUNKS)),
            dma((chips * CHUNKS,)),
        ],
        compiler_params=pltpu.CompilerParams(
            collective_id=0, has_side_effects=True, vmem_limit_bytes=VMEM_BYTES
        ),
        name="gather",
    )(footprints, packet)

    partial = pl.pallas_call(
        functools.partial(spread_kernel, chips),
        out_shape=jax.ShapeDtypeStruct((OBS, OBS), jnp.float32),
        in_specs=[smem, vmem, vmem, vmem],
        out_specs=vmem,
        scratch_shapes=[
            pltpu.VMEM((WEEKS * OBS // TILE, 2 * cells, TILE), jnp.float32),
            pltpu.VMEM((WEEKS, 2 * cells, OBS), jnp.bfloat16),
        ],
        compiler_params=pltpu.CompilerParams(vmem_limit_bytes=VMEM_BYTES),
        name="spread",
    )(meta, tiles, home_tiles, covar)

    return pl.pallas_call(
        functools.partial(reduce_kernel, chips, lines),
        out_shape=jax.ShapeDtypeStruct((rows, OBS), jnp.float32),
        in_specs=[vmem] * 2,
        out_specs=vmem,
        scratch_shapes=[
            pltpu.VMEM((chips, rows, OBS), jnp.float32),
            pltpu.VMEM((depth, rows, OBS), jnp.bfloat16),
            pltpu.VMEM((depth, rows, OBS), jnp.bfloat16),
            pltpu.VMEM((depth, rows, OBS), jnp.bfloat16),
            pltpu.VMEM((2, depth, rows, OBS), jnp.bfloat16),
            dma((chips,)),
            dma((chips,)),
            dma((depth,)),
            dma((depth,)),
            dma((depth,)),
            dma((2, depth)),
        ],
        compiler_params=pltpu.CompilerParams(
            collective_id=1, has_side_effects=True, vmem_limit_bytes=VMEM_BYTES
        ),
        name="reduce",
    )(partial, obs_error.reshape(1, rows))


def solution(mesh):
    placed = (
        P(("groups", "cells"), None, None),
        P(("groups", "cells")),
        P(("groups", "cells")),
        P(("groups", "cells")),
        P(None, ("groups", "cells")),
        P(("groups", "cells")),
    )
    return jax.shard_map(
        local, mesh=mesh, in_specs=placed, out_specs=P(("groups", "cells"), None), check_vma=False
    )
```

```python
import functools

import jax
import jax.numpy as jnp
from jax import lax
from jax.experimental import pallas as pl
from jax.experimental.pallas import tpu as pltpu
from jax.sharding import PartitionSpec as P

WEEKS = 8
OBS = 1024
TILE = 128
SPACE_RANGE = 1.0
TIME_RANGE = 3.0
CHUNKS = 2
VMEM_BYTES = 56 * 1024 * 1024


def place(lines):
    me = lax.axis_index("cells")
    chip = me // 2
    return me, me % 2, chip, chip % lines, chip // lines


def remote(src, dst, send, recv, target):
    return pltpu.make_async_remote_copy(
        src_ref=src,
        dst_ref=dst,
        send_sem=send,
        recv_sem=recv,
        device_id={"cells": target},
        device_id_type=pl.DeviceIdType.MESH,
    )


def signal(sem, target):
    pl.semaphore_signal(
        sem, inc=1, device_id={"cells": target}, device_id_type=pl.DeviceIdType.MESH
    )


def gather_phase(
    chips, lines, own, packet, info, tiles, home_tiles, covar,
    packets, infos, home_pos, pkt_send, pkt_recv, sib_send, sib_recv, hop_send, hop_recv,
    on_places, on_block=None,
):
    depth = chips // lines
    me, core, chip, y, z = place(lines)
    sibling = me + 1 - 2 * core
    slots = own.shape[0]
    part = slots // CHUNKS
    cells = home_pos.shape[1] // 2
    per_dev = cells // TILE

    barrier = pltpu.get_barrier_semaphore()
    for k in range(1, chips):
        signal(barrier, lax.rem(chip + k, chips) * 2 + core)
    signal(barrier, sibling)
    pl.semaphore_wait(barrier, chips)

    pkt_copies = []
    for i, (src, dst) in enumerate(((packet, packets), (info, infos))):
        pkt_copies.append(
            remote(src, dst.at[chips], pkt_send.at[i, 0], pkt_recv.at[i, 0], sibling)
        )
        for k in range(1, chips):
            pkt_copies.append(
                remote(src, dst.at[chip], pkt_send.at[i, k], pkt_recv.at[i, k],
                       lax.rem(chip + k, chips) * 2 + core)
            )
    for copy in pkt_copies:
        copy.start()

    def block(q, ch):
        return tiles.at[pl.ds(q * slots + ch * part, part)]

    sends = []

    def send(cond, kind, step, q, ch, target, first):
        source = own.at[pl.ds(ch * part, part)] if first else block(q, ch)
        copy = remote(source, block(q, ch), hop_send.at[kind, step, ch],
                      hop_recv.at[q * CHUNKS + ch], target)
        sends.append((cond, copy))
        if cond is None:
            copy.start()
        else:
            pl.when(cond)(copy.start)

    def arrive(q, ch):
        remote(block(q, ch), block(q, ch), hop_send.at[0, 0, 0],
               hop_recv.at[q * CHUNKS + ch], sibling).wait_recv()

    above = me + 2 * lines
    below = me - 2 * lines
    across = me + 2 - 4 * y
    for ch in range(CHUNKS):
        send(z < depth - 1, 0, 0, chip, ch, above, True)
        send(z > 0, 1, 0, chip, ch, below, True)
        if lines == 2:
            send(None, 2, 0, chip, ch, across, True)
    sib_copy = remote(own, home_tiles.at[pl.ds(core * slots, slots)], sib_send, sib_recv, sibling)
    sib_copy.start()
    tiles[pl.ds(chip * slots, slots)] = own[...]
    home_tiles[pl.ds(core * slots, slots)] = own[...]
    packets[chip] = packet[...]
    infos[chip] = info[...]

    for copy in pkt_copies:
        copy.wait()

    mine = packet[...]
    other = packets[chips]
    is_first = (core == 0).astype(jnp.float32)
    pair = (mine * is_first + other * (1.0 - is_first), other * is_first + mine * (1.0 - is_first))
    first = jnp.broadcast_to(core == 0, info.shape)
    on_places((
        jnp.where(first, info[...], infos[chips]), jnp.where(first, infos[chips], info[...])
    ))
    for j in range(2):
        columns = jnp.transpose(pair[j])
        for b in range(per_dev):
            rows = pl.ds(j * cells + b * TILE, TILE)
            for axis in range(2):
                col = columns[:, axis * per_dev + b : axis * per_dev + b + 1]
                home_pos[axis, rows, :] = jnp.broadcast_to(col, (TILE, TILE))

    step_rows = 64

    @pl.loop(0, chips)
    def _(q):
        for b in range(per_dev):
            east = packets[q, b : b + 1, :]
            north = packets[q, per_dev + b : per_dev + b + 1, :]

            @pl.loop(0, home_pos.shape[1] // step_rows)
            def _(i):
                rows = pl.ds(i * step_rows, step_rows)
                dx = home_pos[0, rows, :] - east
                dy = home_pos[1, rows, :] - north
                covar[q * per_dev + b, rows, :] = jnp.exp(
                    -jnp.sqrt(dx * dx + dy * dy) / SPACE_RANGE
                ).astype(jnp.bfloat16)

    def done(q, ch):
        if on_block is not None:
            on_block(q, ch)

    def from_across(d, ch):
        def low():
            arrive((z - d) * lines + 1 - y, ch)
            done((z - d) * lines + 1 - y, ch)

        def high():
            arrive((z + d) * lines + 1 - y, ch)
            done((z + d) * lines + 1 - y, ch)

        pl.when(z >= d)(low)
        if d > 0:
            pl.when(z + d < depth)(high)

    for ch in range(CHUNKS):
        done(chip, ch)

    for d in range(1, depth):
        for ch in range(CHUNKS):
            def from_below(d=d, ch=ch):
                arrive((z - d) * lines + y, ch)

            def from_above(d=d, ch=ch):
                arrive((z + d) * lines + y, ch)

            q_low = (z - d) * lines + y
            q_high = (z + d) * lines + y
            pl.when(z >= d)(from_below)
            if d < depth - 1:
                send((z >= d) & (z < depth - 1), 0, d, q_low, ch, above, False)
            if lines == 2:
                send(z >= d, 2, d, q_low, ch, across, False)
            pl.when(z + d < depth)(from_above)
            if d < depth - 1:
                send((z + d < depth) & (z > 0), 1, d, q_high, ch, below, False)
            if lines == 2:
                send(z + d < depth, 3, d, q_high, ch, across, False)
        for ch in range(CHUNKS):
            if on_block is not None:
                pl.when(z >= d)(lambda: on_block((z - d) * lines + y, ch))
                pl.when(z + d < depth)(lambda: on_block((z + d) * lines + y, ch))
        if lines == 2:
            for ch in range(CHUNKS):
                from_across(d - 1, ch)
    if lines == 2:
        for ch in range(CHUNKS):
            from_across(depth - 1, ch)
    for cond, copy in sends:
        if cond is None:
            copy.wait_send()
        else:
            pl.when(cond)(copy.wait_send)
    sib_copy.wait()


def gather_kernel(
    chips, lines, own, packet, info, tiles, home_tiles, covar, meta,
    packets, infos, home_pos, pkt_send, pkt_recv, sib_send, sib_recv, hop_send, hop_recv,
):
    def on_places(pair):
        for q in range(chips):
            meta[q] = infos[q]
        for j in range(2):
            meta[chips + j] = pair[j]

    gather_phase(
        chips, lines, own, packet, info, tiles, home_tiles, covar,
        packets, infos, home_pos, pkt_send, pkt_recv, sib_send, sib_recv, hop_send, hop_recv,
        on_places,
    )


def spread_kernel(chips, meta, tiles, home_tiles, covar, out, acc, weighted):
    slots = tiles.shape[0] // chips
    homes = covar.shape[1]
    cells = homes // 2
    per_dev = cells // TILE
    row_tiles = OBS // TILE

    @pl.loop(0, WEEKS * row_tiles)
    def _(i):
        acc[i] = jnp.zeros((homes, TILE), jnp.float32)

    def place_of(d, s):
        col = meta[d, 0, slots + s]
        return meta[d, 0, s], col // per_dev, col % per_dev

    @pl.loop(0, chips)
    def _(q):
        @pl.loop(0, meta[q, 0, 2 * slots])
        def _(s):
            row, week, b = place_of(q, s)
            strip = covar[q * per_dev + b]
            product = lax.dot_general(
                strip, tiles[q * slots + s], (((1,), (1,)), ((), ())),
                preferred_element_type=jnp.float32,
            )
            acc[week * row_tiles + row] += product

    decay = jnp.exp(jnp.float32(-1.0 / TIME_RANGE))
    step_rows = 16
    for r in range(row_tiles):
        @pl.loop(0, homes // step_rows)
        def _(i):
            rows = pl.ds(i * step_rows, step_rows)
            spread = [acc[w * row_tiles + r, rows, :] for w in range(WEEKS)]
            ahead = [spread[0]]
            for w in range(1, WEEKS):
                ahead.append(spread[w] + decay * ahead[-1])
            back = None
            for w in reversed(range(WEEKS)):
                total = ahead[w] if back is None else ahead[w] + back
                weighted[w, rows, r * TILE : (r + 1) * TILE] = total.astype(jnp.bfloat16)
                back = decay * (spread[w] if back is None else spread[w] + back)

    out[...] = jnp.zeros_like(out)
    for j in range(2):
        @pl.loop(0, meta[chips + j, 0, 2 * slots])
        def _(s):
            row, week, b = place_of(chips + j, s)
            slab = weighted[week, pl.ds(pl.multiple_of(j * cells + b * TILE, TILE), TILE), :]
            product = jnp.dot(
                home_tiles[j * slots + s], slab, preferred_element_type=jnp.float32
            )
            out[pl.ds(pl.multiple_of(row * TILE, TILE), TILE), :] += product


def reduce_phase(
    chips, lines, obs, out, sib, y_out, y_in, z_out, z_in,
    sib_send, sib_recv, y_send, y_recv, z_send, z_recv, outgoing, mine,
):
    depth = chips // lines
    me, core, chip, y, z = place(lines)
    sibling = me + 1 - 2 * core
    rows = out.shape[0]
    above = me + 2 * lines
    below = me - 2 * lines
    across = me + 2 - 4 * y
    up_ok = z < depth - 1
    down_ok = z > 0

    upper = (z >= depth // 2).astype(jnp.int32)

    def order(j):
        if j == depth - 1:
            return z
        high = depth - 1 - j
        high = high - (high <= z).astype(jnp.int32)
        low = j + (j >= z).astype(jnp.int32)
        return upper * low + (1 - upper) * high

    def sib_copy(q):
        return remote(outgoing(q), sib.at[q], sib_send.at[q], sib_recv.at[q], sibling)

    columns = list(reversed(range(lines)))
    for line in columns:
        for j in range(depth):
            sib_copy(order(j) * lines + (y + line) % lines).start()

    def chip_sum(q):
        sib_copy(q).wait_recv()
        return mine(q) + sib[q]

    if lines == 2:
        for j in range(depth):
            c = order(j)
            y_out[c] = chip_sum(c * lines + 1 - y).astype(jnp.bfloat16)
            remote(y_out.at[c], y_in.at[c], y_send.at[c], y_recv.at[c], across).start()

    def up_copy(c):
        return remote(z_out.at[c], z_in.at[0, c], z_send.at[c], z_recv.at[0, c], above)

    def down_copy(c):
        return remote(z_out.at[c], z_in.at[1, c], z_send.at[c], z_recv.at[1, c], below)

    for j in range(depth - 1):
        c = order(j)
        total = chip_sum(c * lines + y)
        if lines == 2:
            remote(y_out.at[c], y_in.at[c], y_send.at[c], y_recv.at[c], across).wait_recv()
            total = total + y_in[c].astype(jnp.float32)
        out[...] = total

        @pl.when((c > z) & down_ok)
        def _():
            up_copy(c).wait_recv()
            out[...] += z_in[0, c].astype(jnp.float32)

        @pl.when((c < z) & up_ok)
        def _():
            down_copy(c).wait_recv()
            out[...] += z_in[1, c].astype(jnp.float32)

        z_out[c] = out[...].astype(jnp.bfloat16)

        @pl.when(c > z)
        def _():
            up_copy(c).start()

        @pl.when(c < z)
        def _():
            down_copy(c).start()

    total = chip_sum(chip)
    if lines == 2:
        remote(y_out.at[z], y_in.at[z], y_send.at[z], y_recv.at[z], across).wait_recv()
        total = total + y_in[z].astype(jnp.float32)
    shape = (rows, rows)
    eye = lax.broadcasted_iota(jnp.int32, shape, 0) == lax.broadcasted_iota(jnp.int32, shape, 1)
    errors = jnp.sum(
        jnp.where(eye, jnp.broadcast_to(obs[...], shape), 0.0), axis=1, keepdims=True
    )
    hit = lax.broadcasted_iota(jnp.int32, out.shape, 1) == (
        me * rows + lax.broadcasted_iota(jnp.int32, out.shape, 0)
    )
    out[...] = total + jnp.where(hit, jnp.broadcast_to(errors, out.shape), 0.0)

    @pl.when(down_ok)
    def _():
        up_copy(z).wait_recv()
        out[...] += z_in[0, z].astype(jnp.float32)

    @pl.when(up_ok)
    def _():
        down_copy(z).wait_recv()
        out[...] += z_in[1, z].astype(jnp.float32)

    for q in range(chips):
        sib_copy(q).wait_send()
    for c in range(depth):
        if lines == 2:
            remote(y_out.at[c], y_in.at[c], y_send.at[c], y_recv.at[c], across).wait_send()
        pl.when(c != z)(lambda c=c: up_copy(c).wait_send())


def reduce_kernel(chips, lines, partial, obs, out, *scratch):
    depth = chips // lines
    me, core, chip, y, z = place(lines)
    rows = out.shape[0]
    above = me + 2 * lines
    below = me - 2 * lines
    up_ok = z < depth - 1
    down_ok = z > 0
    sibling = me + 1 - 2 * core
    across = me + 2 - 4 * y

    barrier = pltpu.get_barrier_semaphore()
    signal(barrier, sibling)
    if lines == 2:
        signal(barrier, across)
    pl.when(up_ok)(lambda: signal(barrier, above))
    pl.when(down_ok)(lambda: signal(barrier, below))
    pl.semaphore_wait(barrier, lines + up_ok.astype(jnp.int32) + down_ok.astype(jnp.int32))

    def slab(q, k):
        return partial.at[pl.ds(pl.multiple_of((q * 2 + k) * rows, 8), rows)]

    reduce_phase(
        chips, lines, obs, out, *scratch,
        lambda q: slab(q, 1 - core), lambda q: slab(q, core)[...],
    )


def sort_tables(key):
    square = (TILE, TILE)
    of_lane = jnp.broadcast_to(key, square)
    of_row = jnp.transpose(of_lane)
    row = lax.broadcasted_iota(jnp.int32, square, 0)
    lane = lax.broadcasted_iota(jnp.int32, square, 1)

    def count(hits):
        return jnp.sum(jnp.where(hits, 1, 0), axis=0, keepdims=True)

    same_before = (of_row == of_lane) & (row < lane)
    rank = count((of_row < of_lane) | same_before)
    repeat = jnp.where(count(same_before) > 0, 1, 0)
    here = jnp.transpose(jnp.broadcast_to(rank, square)) == lane

    def ordered(values):
        column = jnp.transpose(jnp.broadcast_to(values, square))
        return jnp.sum(jnp.where(here, column, 0), axis=0, keepdims=True)

    perm = ordered(lane[0:1, :])
    held = count(of_row == lane)
    end = count(of_row <= lane) - 1
    return ordered, perm, ordered(repeat), end, held


def fused_kernel(
    chips, lines, own, packet, info, obs, out,
    tiles, home_tiles, covar, products, runs, weighted, home_runs, sib_out,
    places, whole_tab, share_tab, whole_s, share_s, tab_sem,
    packets, infos, home_pos, pkt_send, pkt_recv, sib_send, sib_recv, hop_send, hop_recv,
    sib, y_out, y_in, z_out, z_in, ex_send, ex_recv, y_send, y_recv, z_send, z_recv,
):
    slots = own.shape[0]
    part = slots // CHUNKS
    total = chips * slots
    homes = home_pos.shape[1]
    cells = homes // 2
    per_dev = cells // TILE
    row_tiles = OBS // TILE
    rows = out.shape[0]
    core = lax.axis_index("cells") % 2

    def places_of(values):
        n = len(values) * slots
        places[...] = jnp.zeros((TILE, TILE), jnp.int32)
        for i, value in enumerate(values):
            places[i * slots : (i + 1) * slots, :] = jnp.broadcast_to(
                value[0:1, :], (slots, TILE)
            )
        known = jnp.transpose(places[...])
        row = lax.broadcasted_iota(jnp.int32, (TILE, TILE), 0)
        lane = lax.broadcasted_iota(jnp.int32, (TILE, TILE), 1)
        slot = lane % slots

        def pick(at):
            return jnp.sum(jnp.where(row == at, known, 0), axis=0, keepdims=True)

        row_tile, col_tile, count = pick(slot), pick(slots + slot), pick(2 * slots)
        live = (slot[0:1, :] < count) & (lane[0:1, :] < n)
        week = lax.shift_right_logical(col_tile, jnp.full_like(col_tile, per_dev // 2))
        return row_tile, week, col_tile - per_dev * week, live

    def table(row, values):
        whole_tab[row : row + 1, :] = values

    def on_places(pair):
        row_tile, week, cell_block, live = places_of([infos[q] for q in range(chips)])
        key = jnp.where(live, row_tile * WEEKS + week, WEEKS * row_tiles)
        _, perm, keep, end, held = sort_tables(key)
        table(0, perm)
        table(1, jnp.where(held > 0, end, total))
        table(2, cell_block)
        share_tab[0:1, :] = keep.astype(jnp.float32)
        row_tile, week, cell_block, live = places_of(pair)
        key = jnp.where(live, row_tile, row_tiles)
        ordered, perm, keep, end, held = sort_tables(key)
        table(3, perm)
        table(4, jnp.where(held > 0, end, 2 * slots))
        table(5, ordered(week))
        lane = lax.broadcasted_iota(jnp.int32, (1, TILE), 1)
        table(6, ordered(cell_block + jnp.where(lane < slots, 0, per_dev)))
        table(7, jnp.zeros((1, TILE), jnp.int32))
        share_tab[1:2, :] = keep.astype(jnp.float32)
        share_tab[2:8, :] = jnp.zeros((6, TILE), jnp.float32)
        for i, (src, dst) in enumerate(((whole_tab, whole_s), (share_tab, share_s))):
            copy = pltpu.make_async_copy(src, dst, tab_sem.at[i])
            copy.start()
            copy.wait()

    def on_block(q, ch):
        @pl.loop(0, part)
        def _(s):
            t = q * slots + ch * part + s
            products[t] = lax.dot_general(
                covar[q * per_dev + whole_s[2, t]], tiles[t], (((1,), (1,)), ((), ())),
                preferred_element_type=jnp.float32,
            )

    gather_phase(
        chips, lines, own, packet, info, tiles, home_tiles, covar,
        packets, infos, home_pos, pkt_send, pkt_recv, sib_send, sib_recv, hop_send, hop_recv,
        on_places, on_block,
    )

    decay = jnp.exp(jnp.float32(-1.0 / TIME_RANGE))
    step_rows = runs.shape[1]
    runs[total] = jnp.zeros((step_rows, TILE), jnp.float32)

    steps = TILE // step_rows

    @pl.loop(0, homes // step_rows)
    def _(i):
        strip = pl.ds(pl.multiple_of(i * step_rows, step_rows), step_rows)
        inner = pl.ds(pl.multiple_of((i % steps) * step_rows, step_rows), step_rows)
        running = jnp.zeros((step_rows, TILE), jnp.float32)
        for n in range(total):
            running = running * share_s[0, n] + products[whole_s[0, n], strip, :]
            runs[n] = running
        for r in range(row_tiles):
            spread = [runs[whole_s[1, r * WEEKS + w]] for w in range(WEEKS)]
            ahead = [spread[0]]
            for w in range(1, WEEKS):
                ahead.append(spread[w] + decay * ahead[-1])
            back = None
            for w in reversed(range(WEEKS)):
                value = ahead[w] if back is None else ahead[w] + back
                weighted[w, i // steps, inner, r * TILE : (r + 1) * TILE] = value.astype(jnp.bfloat16)
                back = decay * (spread[w] if back is None else spread[w] + back)

    home_runs[2 * slots] = jnp.zeros((TILE, OBS), jnp.float32)

    @pl.loop(0, 2 * slots)
    def _(n):
        value = jnp.dot(
            home_tiles[whole_s[3, n]], weighted[whole_s[5, n], whole_s[6, n]],
            preferred_element_type=jnp.float32,
        )
        before = home_runs[lax.rem(n + 2 * slots, 2 * slots + 1)]
        home_runs[n] = value + before * share_s[1, n]

    def half(q, k):
        return home_runs[whole_s[4, q], pl.ds(pl.multiple_of(k * rows, 8), rows), :]

    for q in range(chips):
        sib_out[q] = half(q, 1 - core)

    reduce_phase(
        chips, lines, obs, out, sib, y_out, y_in, z_out, z_in,
        ex_send, ex_recv, y_send, y_recv, z_send, z_recv,
        lambda q: sib_out.at[q], lambda q: half(q, core),
    )


def local(footprints, tile_rows, tile_cols, tile_counts, coords, obs_error):
    count = lax.axis_size("cells")
    chips = count // 2
    lines = 2 if chips == 8 else 1
    depth = chips // lines
    slots = footprints.shape[0]
    cells = coords.shape[1]
    per_dev = cells // TILE
    rows = OBS // count
    vmem = pl.BlockSpec(memory_space=pltpu.VMEM)
    smem = pl.BlockSpec(memory_space=pltpu.SMEM)
    dma = pltpu.SemaphoreType.DMA

    info = jnp.concatenate([tile_rows, tile_cols, tile_counts])
    info = jnp.pad(info[None, :], ((0, 7), (0, TILE - info.shape[0])))
    packet = coords.reshape(2 * per_dev, TILE)
    packet = jnp.pad(packet, ((0, 8 - packet.shape[0]), (0, 0)))

    f32, bf16 = jnp.float32, jnp.bfloat16
    gather_scratch = [
        pltpu.VMEM((chips + 1, 8, TILE), f32),
        pltpu.VMEM((chips + 1, 8, TILE), jnp.int32),
        pltpu.VMEM((2, 2 * cells, TILE), f32),
        dma((2, chips)),
        dma((2, chips)),
        dma,
        dma,
        dma((4, depth, CHUNKS)),
        dma((chips * CHUNKS,)),
    ]
    reduce_scratch = [
        pltpu.VMEM((chips, rows, OBS), f32),
        pltpu.VMEM((depth, rows, OBS), bf16),
        pltpu.VMEM((depth, rows, OBS), bf16),
        pltpu.VMEM((depth, rows, OBS), bf16),
        pltpu.VMEM((2, depth, rows, OBS), bf16),
        dma((chips,)),
        dma((chips,)),
        dma((depth,)),
        dma((depth,)),
        dma((depth,)),
        dma((2, depth)),
    ]
    if chips * slots < TILE and chips * TILE == OBS:
        total = chips * slots
        return pl.pallas_call(
            functools.partial(fused_kernel, chips, lines),
            out_shape=jax.ShapeDtypeStruct((rows, OBS), f32),
            in_specs=[vmem] * 4,
            out_specs=vmem,
            scratch_shapes=[
                pltpu.VMEM((total, TILE, TILE), bf16),
                pltpu.VMEM((2 * slots, TILE, TILE), bf16),
                pltpu.VMEM((chips * per_dev, 2 * cells, TILE), bf16),
                pltpu.VMEM((total, 2 * cells, TILE), f32),
                pltpu.VMEM((total + 1, 32, TILE), f32),
                pltpu.VMEM((WEEKS, 2 * per_dev, TILE, OBS), bf16),
                pltpu.VMEM((2 * slots + 1, TILE, OBS), f32),
                pltpu.VMEM((chips, rows, OBS), f32),
                pltpu.VMEM((TILE, TILE), jnp.int32),
                pltpu.VMEM((8, TILE), jnp.int32),
                pltpu.VMEM((8, TILE), f32),
                pltpu.SMEM((8, TILE), jnp.int32),
                pltpu.SMEM((8, TILE), f32),
                dma((2,)),
                *gather_scratch,
                *reduce_scratch,
            ],
            compiler_params=pltpu.CompilerParams(
                collective_id=0, has_side_effects=True, vmem_limit_bytes=VMEM_BYTES
            ),
            name="fused",
        )(footprints, packet, info, obs_error.reshape(1, rows))

    tiles, home_tiles, covar, meta = pl.pallas_call(
        functools.partial(gather_kernel, chips, lines),
        out_shape=(
            jax.ShapeDtypeStruct((chips * slots, TILE, TILE), bf16),
            jax.ShapeDtypeStruct((2 * slots, TILE, TILE), bf16),
            jax.ShapeDtypeStruct((chips * per_dev, 2 * cells, TILE), bf16),
            jax.ShapeDtypeStruct((chips + 2, 8, TILE), jnp.int32),
        ),
        in_specs=[vmem] * 3,
        out_specs=(vmem,) * 4,
        scratch_shapes=gather_scratch,
        compiler_params=pltpu.CompilerParams(
            collective_id=0, has_side_effects=True, vmem_limit_bytes=VMEM_BYTES
        ),
        name="gather",
    )(footprints, packet, info)

    partial = pl.pallas_call(
        functools.partial(spread_kernel, chips),
        out_shape=jax.ShapeDtypeStruct((OBS, OBS), jnp.float32),
        in_specs=[smem, vmem, vmem, vmem],
        out_specs=vmem,
        scratch_shapes=[
            pltpu.VMEM((WEEKS * OBS // TILE, 2 * cells, TILE), jnp.float32),
            pltpu.VMEM((WEEKS, 2 * cells, OBS), jnp.bfloat16),
        ],
        compiler_params=pltpu.CompilerParams(vmem_limit_bytes=VMEM_BYTES),
        name="spread",
    )(meta, tiles, home_tiles, covar)

    return pl.pallas_call(
        functools.partial(reduce_kernel, chips, lines),
        out_shape=jax.ShapeDtypeStruct((rows, OBS), f32),
        in_specs=[vmem] * 2,
        out_specs=vmem,
        scratch_shapes=reduce_scratch,
        compiler_params=pltpu.CompilerParams(
            collective_id=1, has_side_effects=True, vmem_limit_bytes=VMEM_BYTES
        ),
        name="reduce",
    )(partial, obs_error.reshape(1, rows))


def solution(mesh):
    placed = (
        P(("groups", "cells"), None, None),
        P(("groups", "cells")),
        P(("groups", "cells")),
        P(("groups", "cells")),
        P(None, ("groups", "cells")),
        P(("groups", "cells")),
    )
    return jax.shard_map(
        local, mesh=mesh, in_specs=placed, out_specs=P(("groups", "cells"), None), check_vma=False
    )
```

```python
import functools

import jax
import jax.numpy as jnp
from jax import lax
from jax.experimental import pallas as pl
from jax.experimental.pallas import tpu as pltpu
from jax.sharding import PartitionSpec as P

WEEKS = 8
OBS = 1024
TILE = 128
SPACE_RANGE = 1.0
TIME_RANGE = 3.0
CHUNKS = 2
SPLIT = 2
VMEM_BYTES = 56 * 1024 * 1024


def place(lines):
    me = lax.axis_index("cells")
    chip = me // 2
    return me, me % 2, chip, chip % lines, chip // lines


def remote(src, dst, send, recv, target):
    return pltpu.make_async_remote_copy(
        src_ref=src,
        dst_ref=dst,
        send_sem=send,
        recv_sem=recv,
        device_id={"cells": target},
        device_id_type=pl.DeviceIdType.MESH,
    )


def signal(sem, target):
    pl.semaphore_signal(
        sem, inc=1, device_id={"cells": target}, device_id_type=pl.DeviceIdType.MESH
    )


def gather_phase(
    chips, lines, own, coords, raw, tiles, home_tiles, covar,
    packet, info, packets, infos, home_pos, pkt_send, pkt_recv, sib_send, sib_recv, hop_send, hop_recv,
    on_places, on_block=None,
):
    depth = chips // lines
    me, core, chip, y, z = place(lines)
    sibling = me + 1 - 2 * core
    slots = own.shape[0]
    part = slots // CHUNKS
    cells = home_pos.shape[1] // 2
    per_dev = cells // TILE

    barrier = pltpu.get_barrier_semaphore()
    for k in range(1, chips):
        signal(barrier, lax.rem(chip + k, chips) * 2 + core)
    signal(barrier, sibling)
    pl.semaphore_wait(barrier, chips)

    packet[...] = jnp.zeros_like(packet)
    for axis in range(2):
        for b in range(per_dev):
            packet[axis * per_dev + b : axis * per_dev + b + 1, :] = coords[
                axis : axis + 1, b * TILE : (b + 1) * TILE
            ]
    info[...] = jnp.zeros_like(info)
    for i, ref in enumerate(raw):
        info[i : i + 1, 0 : ref.shape[1]] = ref[...]

    pkt_copies = []
    for i, (src, dst) in enumerate(((packet, packets), (info, infos))):
        pkt_copies.append(
            remote(src, dst.at[chips], pkt_send.at[i, 0], pkt_recv.at[i, 0], sibling)
        )
        for k in range(1, chips):
            pkt_copies.append(
                remote(src, dst.at[chip], pkt_send.at[i, k], pkt_recv.at[i, k],
                       lax.rem(chip + k, chips) * 2 + core)
            )
    for copy in pkt_copies:
        copy.start()

    def block(q, ch):
        return tiles.at[pl.ds(q * slots + ch * part, part)]

    sends = []

    def send(cond, kind, step, q, ch, target, first):
        source = own.at[pl.ds(ch * part, part)] if first else block(q, ch)
        copy = remote(source, block(q, ch), hop_send.at[kind, step, ch],
                      hop_recv.at[q * CHUNKS + ch], target)
        sends.append((cond, copy))
        if cond is None:
            copy.start()
        else:
            pl.when(cond)(copy.start)

    def arrive(q, ch):
        remote(block(q, ch), block(q, ch), hop_send.at[0, 0, 0],
               hop_recv.at[q * CHUNKS + ch], sibling).wait_recv()

    above = me + 2 * lines
    below = me - 2 * lines
    across = me + 2 - 4 * y
    for ch in range(CHUNKS):
        send(z < depth - 1, 0, 0, chip, ch, above, True)
        send(z > 0, 1, 0, chip, ch, below, True)
        if lines == 2:
            send(None, 2, 0, chip, ch, across, True)
    sib_copy = remote(own, home_tiles.at[pl.ds(core * slots, slots)], sib_send, sib_recv, sibling)
    sib_copy.start()
    tiles[pl.ds(chip * slots, slots)] = own[...]
    home_tiles[pl.ds(core * slots, slots)] = own[...]
    packets[chip] = packet[...]
    infos[chip] = info[...]

    for copy in pkt_copies:
        copy.wait()

    mine = packet[...]
    other = packets[chips]
    is_first = (core == 0).astype(jnp.float32)
    pair = (mine * is_first + other * (1.0 - is_first), other * is_first + mine * (1.0 - is_first))
    first = jnp.broadcast_to(core == 0, info.shape)
    on_places((
        jnp.where(first, info[...], infos[chips]), jnp.where(first, infos[chips], info[...])
    ))
    for j in range(2):
        columns = jnp.transpose(pair[j])
        for b in range(per_dev):
            rows = pl.ds(j * cells + b * TILE, TILE)
            for axis in range(2):
                col = columns[:, axis * per_dev + b : axis * per_dev + b + 1]
                home_pos[axis, rows, :] = jnp.broadcast_to(col, (TILE, TILE))

    step_rows = 64

    @pl.loop(0, chips)
    def _(q):
        for b in range(per_dev):
            east = packets[q, b : b + 1, :]
            north = packets[q, per_dev + b : per_dev + b + 1, :]

            @pl.loop(0, home_pos.shape[1] // step_rows)
            def _(i):
                rows = pl.ds(i * step_rows, step_rows)
                dx = home_pos[0, rows, :] - east
                dy = home_pos[1, rows, :] - north
                covar[q * per_dev + b, rows, :] = jnp.exp(
                    -jnp.sqrt(dx * dx + dy * dy) / SPACE_RANGE
                ).astype(jnp.bfloat16)

    def done(q, ch):
        if on_block is not None:
            on_block(q, ch)

    def from_across(d, ch):
        def low():
            arrive((z - d) * lines + 1 - y, ch)
            done((z - d) * lines + 1 - y, ch)

        def high():
            arrive((z + d) * lines + 1 - y, ch)
            done((z + d) * lines + 1 - y, ch)

        pl.when(z >= d)(low)
        if d > 0:
            pl.when(z + d < depth)(high)

    for ch in range(CHUNKS):
        done(chip, ch)

    for d in range(1, depth):
        for ch in range(CHUNKS):
            def from_below(d=d, ch=ch):
                arrive((z - d) * lines + y, ch)

            def from_above(d=d, ch=ch):
                arrive((z + d) * lines + y, ch)

            q_low = (z - d) * lines + y
            q_high = (z + d) * lines + y
            pl.when(z >= d)(from_below)
            if d < depth - 1:
                send((z >= d) & (z < depth - 1), 0, d, q_low, ch, above, False)
            if lines == 2:
                send(z >= d, 2, d, q_low, ch, across, False)
            pl.when(z + d < depth)(from_above)
            if d < depth - 1:
                send((z + d < depth) & (z > 0), 1, d, q_high, ch, below, False)
            if lines == 2:
                send(z + d < depth, 3, d, q_high, ch, across, False)
        for ch in range(CHUNKS):
            if on_block is not None:
                pl.when(z >= d)(lambda: on_block((z - d) * lines + y, ch))
                pl.when(z + d < depth)(lambda: on_block((z + d) * lines + y, ch))
        if lines == 2:
            for ch in range(CHUNKS):
                from_across(d - 1, ch)
    if lines == 2:
        for ch in range(CHUNKS):
            from_across(depth - 1, ch)
    for cond, copy in sends:
        if cond is None:
            copy.wait_send()
        else:
            pl.when(cond)(copy.wait_send)
    sib_copy.wait()


def gather_kernel(
    chips, lines, own, coords, row_in, col_in, count_in, tiles, home_tiles, covar, meta,
    packet, info, packets, infos, home_pos, pkt_send, pkt_recv, sib_send, sib_recv, hop_send, hop_recv,
):
    def on_places(pair):
        for q in range(chips):
            meta[q] = infos[q]
        for j in range(2):
            meta[chips + j] = pair[j]

    gather_phase(
        chips, lines, own, coords, (row_in, col_in, count_in), tiles, home_tiles, covar,
        packet, info, packets, infos, home_pos, pkt_send, pkt_recv, sib_send, sib_recv, hop_send, hop_recv,
        on_places,
    )


def spread_kernel(chips, meta, tiles, home_tiles, covar, out, acc, weighted):
    slots = tiles.shape[0] // chips
    homes = covar.shape[1]
    cells = homes // 2
    per_dev = cells // TILE
    row_tiles = OBS // TILE

    @pl.loop(0, WEEKS * row_tiles)
    def _(i):
        acc[i] = jnp.zeros((homes, TILE), jnp.float32)

    def place_of(d, s):
        col = meta[d, 1, s]
        return meta[d, 0, s], col // per_dev, col % per_dev

    @pl.loop(0, chips)
    def _(q):
        @pl.loop(0, meta[q, 2, 0])
        def _(s):
            row, week, b = place_of(q, s)
            strip = covar[q * per_dev + b]
            product = lax.dot_general(
                strip, tiles[q * slots + s], (((1,), (1,)), ((), ())),
                preferred_element_type=jnp.float32,
            )
            acc[week * row_tiles + row] += product

    decay = jnp.exp(jnp.float32(-1.0 / TIME_RANGE))
    step_rows = 16
    for r in range(row_tiles):
        @pl.loop(0, homes // step_rows)
        def _(i):
            rows = pl.ds(i * step_rows, step_rows)
            spread = [acc[w * row_tiles + r, rows, :] for w in range(WEEKS)]
            ahead = [spread[0]]
            for w in range(1, WEEKS):
                ahead.append(spread[w] + decay * ahead[-1])
            back = None
            for w in reversed(range(WEEKS)):
                total = ahead[w] if back is None else ahead[w] + back
                weighted[w, rows, r * TILE : (r + 1) * TILE] = total.astype(jnp.bfloat16)
                back = decay * (spread[w] if back is None else spread[w] + back)

    out[...] = jnp.zeros_like(out)
    for j in range(2):
        @pl.loop(0, meta[chips + j, 2, 0])
        def _(s):
            row, week, b = place_of(chips + j, s)
            slab = weighted[week, pl.ds(pl.multiple_of(j * cells + b * TILE, TILE), TILE), :]
            product = jnp.dot(
                home_tiles[j * slots + s], slab, preferred_element_type=jnp.float32
            )
            out[pl.ds(pl.multiple_of(row * TILE, TILE), TILE), :] += product


def reduce_phase(
    chips, lines, obs, out, sib, y_out, y_in, z_out, z_in,
    sib_send, sib_recv, y_send, y_recv, z_send, z_recv, prepare, outgoing, mine,
):
    depth = chips // lines
    me, core, chip, y, z = place(lines)
    sibling = me + 1 - 2 * core
    rows = out.shape[0]
    width = out.shape[1] // SPLIT
    above = me + 2 * lines
    below = me - 2 * lines
    across = me + 2 - 4 * y
    up_ok = z < depth - 1
    down_ok = z > 0
    upper = (z >= depth // 2).astype(jnp.int32)

    def order(j):
        if j == depth - 1:
            return z
        high = depth - 1 - j
        high = high - (high <= z).astype(jnp.int32)
        low = j + (j >= z).astype(jnp.int32)
        return upper * low + (1 - upper) * high

    def sib_copy(h, q):
        return remote(
            outgoing(h, q), sib.at[h, q], sib_send.at[h, q], sib_recv.at[h, q], sibling
        )

    def chip_sum(h, q):
        sib_copy(h, q).wait_recv()
        return mine(h, q) + sib[h, q]

    def y_copy(h, c):
        return remote(y_out.at[h, c], y_in.at[h, c], y_send.at[h, c], y_recv.at[h, c], across)

    def up_copy(h, c):
        return remote(z_out.at[h, c], z_in.at[h, 0, c], z_send.at[h, c], z_recv.at[h, 0, c], above)

    def down_copy(h, c):
        return remote(z_out.at[h, c], z_in.at[h, 1, c], z_send.at[h, c], z_recv.at[h, 1, c], below)

    def y_stage(h):
        for j in range(depth):
            c = order(j)
            y_out[h, c] = chip_sum(h, c * lines + 1 - y).astype(jnp.bfloat16)
            y_copy(h, c).start()

    for h in range(SPLIT):
        prepare(h)
        for line in reversed(range(lines)):
            for j in range(depth):
                sib_copy(h, order(j) * lines + (y + line) % lines).start()
        if lines == 2 and h > 0:
            y_stage(h - 1)
    if lines == 2:
        y_stage(SPLIT - 1)

    def column_sum(h, c):
        total = chip_sum(h, c * lines + y)
        if lines == 2:
            y_copy(h, c).wait_recv()
            total = total + y_in[h, c].astype(jnp.float32)
        return total

    for j in range(depth - 1):
        for h in range(SPLIT):
            c = order(j)
            part = (slice(None), slice(h * width, (h + 1) * width))
            out[part] = column_sum(h, c)

            @pl.when((c > z) & down_ok)
            def _():
                up_copy(h, c).wait_recv()
                out[part] += z_in[h, 0, c].astype(jnp.float32)

            @pl.when((c < z) & up_ok)
            def _():
                down_copy(h, c).wait_recv()
                out[part] += z_in[h, 1, c].astype(jnp.float32)

            z_out[h, c] = out[part].astype(jnp.bfloat16)

            @pl.when(c > z)
            def _():
                up_copy(h, c).start()

            @pl.when(c < z)
            def _():
                down_copy(h, c).start()

    shape = (rows, rows)
    eye = lax.broadcasted_iota(jnp.int32, shape, 0) == lax.broadcasted_iota(jnp.int32, shape, 1)
    errors = jnp.sum(
        jnp.where(eye, jnp.broadcast_to(obs[...], shape), 0.0), axis=1, keepdims=True
    )
    for h in range(SPLIT):
        part = (slice(None), slice(h * width, (h + 1) * width))
        block = (rows, width)
        hit = h * width + lax.broadcasted_iota(jnp.int32, block, 1) == (
            me * rows + lax.broadcasted_iota(jnp.int32, block, 0)
        )
        out[part] = column_sum(h, z) + jnp.where(hit, jnp.broadcast_to(errors, block), 0.0)

        @pl.when(down_ok)
        def _():
            up_copy(h, z).wait_recv()
            out[part] += z_in[h, 0, z].astype(jnp.float32)

        @pl.when(up_ok)
        def _():
            down_copy(h, z).wait_recv()
            out[part] += z_in[h, 1, z].astype(jnp.float32)

    for h in range(SPLIT):
        for q in range(chips):
            sib_copy(h, q).wait_send()
        for c in range(depth):
            if lines == 2:
                y_copy(h, c).wait_send()
            pl.when(c != z)(lambda: up_copy(h, c).wait_send())


def reduce_kernel(chips, lines, partial, obs, out, *scratch):
    depth = chips // lines
    me, core, chip, y, z = place(lines)
    rows = out.shape[0]
    above = me + 2 * lines
    below = me - 2 * lines
    up_ok = z < depth - 1
    down_ok = z > 0
    sibling = me + 1 - 2 * core
    across = me + 2 - 4 * y

    barrier = pltpu.get_barrier_semaphore()
    signal(barrier, sibling)
    if lines == 2:
        signal(barrier, across)
    pl.when(up_ok)(lambda: signal(barrier, above))
    pl.when(down_ok)(lambda: signal(barrier, below))
    pl.semaphore_wait(barrier, lines + up_ok.astype(jnp.int32) + down_ok.astype(jnp.int32))

    width = out.shape[1] // SPLIT

    def slab(h, q, k):
        return partial.at[
            pl.ds(pl.multiple_of((q * 2 + k) * rows, 8), rows), pl.ds(h * width, width)
        ]

    reduce_phase(
        chips, lines, obs, out, *scratch,
        lambda h: None, lambda h, q: slab(h, q, 1 - core), lambda h, q: slab(h, q, core)[...],
    )


def sort_tables(key):
    square = (TILE, TILE)
    of_lane = jnp.broadcast_to(key, square)
    of_row = jnp.transpose(of_lane)
    row = lax.broadcasted_iota(jnp.int32, square, 0)
    lane = lax.broadcasted_iota(jnp.int32, square, 1)

    def count(hits):
        return jnp.sum(jnp.where(hits, 1, 0), axis=0, keepdims=True)

    same_before = (of_row == of_lane) & (row < lane)
    rank = count((of_row < of_lane) | same_before)
    repeat = jnp.where(count(same_before) > 0, 1, 0)
    here = jnp.transpose(jnp.broadcast_to(rank, square)) == lane

    def ordered(values):
        column = jnp.transpose(jnp.broadcast_to(values, square))
        return jnp.sum(jnp.where(here, column, 0), axis=0, keepdims=True)

    perm = ordered(lane[0:1, :])
    held = count(of_row == lane)
    end = count(of_row <= lane) - 1
    return ordered, perm, ordered(repeat), end, held


def fused_kernel(
    chips, lines, own, coords, row_in, col_in, count_in, obs, out,
    tiles, home_tiles, covar, products, runs, weighted, home_runs, sib_out,
    places, whole_tab, share_tab, whole_s, share_s, tab_sem,
    packet, info, packets, infos, home_pos, pkt_send, pkt_recv, sib_send, sib_recv, hop_send, hop_recv,
    sib, y_out, y_in, z_out, z_in, ex_send, ex_recv, y_send, y_recv, z_send, z_recv,
):
    slots = own.shape[0]
    part = slots // CHUNKS
    total = chips * slots
    homes = home_pos.shape[1]
    cells = homes // 2
    per_dev = cells // TILE
    row_tiles = OBS // TILE
    rows = out.shape[0]
    core = lax.axis_index("cells") % 2

    def places_of(values):
        n = len(values) * slots
        row = lax.broadcasted_iota(jnp.int32, (TILE, TILE), 0)
        lane = lax.broadcasted_iota(jnp.int32, (TILE, TILE), 1)
        slot = lane % slots
        picked = []
        for k, at in enumerate((slot, slot, 0)):
            places[k] = jnp.zeros((TILE, TILE), jnp.int32)
            for i, value in enumerate(values):
                places[k, i * slots : (i + 1) * slots, :] = jnp.broadcast_to(
                    value[k : k + 1, :], (slots, TILE)
                )
            known = jnp.transpose(places[k])
            picked.append(jnp.sum(jnp.where(row == at, known, 0), axis=0, keepdims=True))
        row_tile, col_tile, count = picked
        live = (slot[0:1, :] < count) & (lane[0:1, :] < n)
        week = lax.shift_right_logical(col_tile, jnp.full_like(col_tile, per_dev // 2))
        return row_tile, week, col_tile - per_dev * week, live

    def table(row, values):
        whole_tab[row : row + 1, :] = values

    def on_places(pair):
        row_tile, week, cell_block, live = places_of([infos[q] for q in range(chips)])
        key = jnp.where(live, row_tile * WEEKS + week, WEEKS * row_tiles)
        _, perm, keep, end, held = sort_tables(key)
        table(0, perm)
        table(1, jnp.where(held > 0, end, total))
        table(2, cell_block)
        share_tab[0:1, :] = keep.astype(jnp.float32)
        row_tile, week, cell_block, live = places_of(pair)
        key = jnp.where(live, row_tile, row_tiles)
        ordered, perm, keep, end, held = sort_tables(key)
        table(3, perm)
        table(4, jnp.where(held > 0, end, 2 * slots))
        table(5, ordered(week))
        lane = lax.broadcasted_iota(jnp.int32, (1, TILE), 1)
        table(6, ordered(cell_block + jnp.where(lane < slots, 0, per_dev)))
        table(7, jnp.zeros((1, TILE), jnp.int32))
        share_tab[1:2, :] = keep.astype(jnp.float32)
        share_tab[2:8, :] = jnp.zeros((6, TILE), jnp.float32)
        for i, (src, dst) in enumerate(((whole_tab, whole_s), (share_tab, share_s))):
            copy = pltpu.make_async_copy(src, dst, tab_sem.at[i])
            copy.start()
            copy.wait()

    def on_block(q, ch):
        @pl.loop(0, part)
        def _(s):
            t = q * slots + ch * part + s
            products[t] = lax.dot_general(
                covar[q * per_dev + whole_s[2, t]], tiles[t], (((1,), (1,)), ((), ())),
                preferred_element_type=jnp.float32,
            )

    gather_phase(
        chips, lines, own, coords, (row_in, col_in, count_in), tiles, home_tiles, covar,
        packet, info, packets, infos, home_pos, pkt_send, pkt_recv, sib_send, sib_recv, hop_send, hop_recv,
        on_places, on_block,
    )

    decay = jnp.exp(jnp.float32(-1.0 / TIME_RANGE))
    step_rows = runs.shape[1]
    runs[total] = jnp.zeros((step_rows, TILE), jnp.float32)

    steps = TILE // step_rows

    @pl.loop(0, homes // step_rows)
    def _(i):
        strip = pl.ds(pl.multiple_of(i * step_rows, step_rows), step_rows)
        inner = pl.ds(pl.multiple_of((i % steps) * step_rows, step_rows), step_rows)
        running = jnp.zeros((step_rows, TILE), jnp.float32)
        for n in range(total):
            running = running * share_s[0, n] + products[whole_s[0, n], strip, :]
            runs[n] = running
        for r in range(row_tiles):
            spread = [runs[whole_s[1, r * WEEKS + w]] for w in range(WEEKS)]
            ahead = [spread[0]]
            for w in range(1, WEEKS):
                ahead.append(spread[w] + decay * ahead[-1])
            back = None
            for w in reversed(range(WEEKS)):
                value = ahead[w] if back is None else ahead[w] + back
                weighted[w, i // steps, inner, r * TILE : (r + 1) * TILE] = value.astype(jnp.bfloat16)
                back = decay * (spread[w] if back is None else spread[w] + back)

    width = OBS // SPLIT

    def half(h, q, k):
        return home_runs[h, whole_s[4, q], pl.ds(pl.multiple_of(k * rows, 8), rows), :]

    def prepare(h):
        home_runs[h, 2 * slots] = jnp.zeros((TILE, width), jnp.float32)

        @pl.loop(0, 2 * slots, unroll=4)
        def _(n):
            value = jnp.dot(
                home_tiles[whole_s[3, n]],
                weighted[whole_s[5, n], whole_s[6, n], :, pl.ds(h * width, width)],
                preferred_element_type=jnp.float32,
            )
            before = home_runs[h, lax.rem(n + 2 * slots, 2 * slots + 1)]
            home_runs[h, n] = value + before * share_s[1, n]

        for q in range(chips):
            sib_out[h, q] = half(h, q, 1 - core)

    reduce_phase(
        chips, lines, obs, out, sib, y_out, y_in, z_out, z_in,
        ex_send, ex_recv, y_send, y_recv, z_send, z_recv,
        prepare, lambda h, q: sib_out.at[h, q], lambda h, q: half(h, q, core),
    )


def local(footprints, tile_rows, tile_cols, tile_counts, coords, obs_error):
    count = lax.axis_size("cells")
    chips = count // 2
    lines = 2 if chips == 8 else 1
    depth = chips // lines
    slots = footprints.shape[0]
    cells = coords.shape[1]
    per_dev = cells // TILE
    rows = OBS // count
    vmem = pl.BlockSpec(memory_space=pltpu.VMEM)
    smem = pl.BlockSpec(memory_space=pltpu.SMEM)
    dma = pltpu.SemaphoreType.DMA

    places = (
        tile_rows.reshape(1, slots), tile_cols.reshape(1, slots), tile_counts.reshape(1, 1)
    )
    f32, bf16 = jnp.float32, jnp.bfloat16
    gather_scratch = [
        pltpu.VMEM((8, TILE), f32),
        pltpu.VMEM((8, TILE), jnp.int32),
        pltpu.VMEM((chips + 1, 8, TILE), f32),
        pltpu.VMEM((chips + 1, 8, TILE), jnp.int32),
        pltpu.VMEM((2, 2 * cells, TILE), f32),
        dma((2, chips)),
        dma((2, chips)),
        dma,
        dma,
        dma((4, depth, CHUNKS)),
        dma((chips * CHUNKS,)),
    ]
    width = OBS // SPLIT
    reduce_scratch = [
        pltpu.VMEM((SPLIT, chips, rows, width), f32),
        pltpu.VMEM((SPLIT, depth, rows, width), bf16),
        pltpu.VMEM((SPLIT, depth, rows, width), bf16),
        pltpu.VMEM((SPLIT, depth, rows, width), bf16),
        pltpu.VMEM((SPLIT, 2, depth, rows, width), bf16),
        dma((SPLIT, chips)),
        dma((SPLIT, chips)),
        dma((SPLIT, depth)),
        dma((SPLIT, depth)),
        dma((SPLIT, depth)),
        dma((SPLIT, 2, depth)),
    ]
    if chips * slots < TILE and chips * TILE == OBS:
        total = chips * slots
        return pl.pallas_call(
            functools.partial(fused_kernel, chips, lines),
            out_shape=jax.ShapeDtypeStruct((rows, OBS), f32),
            in_specs=[vmem] * 6,
            out_specs=vmem,
            scratch_shapes=[
                pltpu.VMEM((total, TILE, TILE), bf16),
                pltpu.VMEM((2 * slots, TILE, TILE), bf16),
                pltpu.VMEM((chips * per_dev, 2 * cells, TILE), bf16),
                pltpu.VMEM((total, 2 * cells, TILE), f32),
                pltpu.VMEM((total + 1, 32, TILE), f32),
                pltpu.VMEM((WEEKS, 2 * per_dev, TILE, OBS), bf16),
                pltpu.VMEM((SPLIT, 2 * slots + 1, TILE, width), f32),
                pltpu.VMEM((SPLIT, chips, rows, width), f32),
                pltpu.VMEM((3, TILE, TILE), jnp.int32),
                pltpu.VMEM((8, TILE), jnp.int32),
                pltpu.VMEM((8, TILE), f32),
                pltpu.SMEM((8, TILE), jnp.int32),
                pltpu.SMEM((8, TILE), f32),
                dma((2,)),
                *gather_scratch,
                *reduce_scratch,
            ],
            compiler_params=pltpu.CompilerParams(
                collective_id=0, has_side_effects=True, vmem_limit_bytes=VMEM_BYTES
            ),
            name="fused",
        )(footprints, coords, *places, obs_error.reshape(1, rows))

    tiles, home_tiles, covar, meta = pl.pallas_call(
        functools.partial(gather_kernel, chips, lines),
        out_shape=(
            jax.ShapeDtypeStruct((chips * slots, TILE, TILE), bf16),
            jax.ShapeDtypeStruct((2 * slots, TILE, TILE), bf16),
            jax.ShapeDtypeStruct((chips * per_dev, 2 * cells, TILE), bf16),
            jax.ShapeDtypeStruct((chips + 2, 8, TILE), jnp.int32),
        ),
        in_specs=[vmem] * 5,
        out_specs=(vmem,) * 4,
        scratch_shapes=gather_scratch,
        compiler_params=pltpu.CompilerParams(
            collective_id=0, has_side_effects=True, vmem_limit_bytes=VMEM_BYTES
        ),
        name="gather",
    )(footprints, coords, *places)

    partial = pl.pallas_call(
        functools.partial(spread_kernel, chips),
        out_shape=jax.ShapeDtypeStruct((OBS, OBS), jnp.float32),
        in_specs=[smem, vmem, vmem, vmem],
        out_specs=vmem,
        scratch_shapes=[
            pltpu.VMEM((WEEKS * OBS // TILE, 2 * cells, TILE), jnp.float32),
            pltpu.VMEM((WEEKS, 2 * cells, OBS), jnp.bfloat16),
        ],
        compiler_params=pltpu.CompilerParams(vmem_limit_bytes=VMEM_BYTES),
        name="spread",
    )(meta, tiles, home_tiles, covar)

    return pl.pallas_call(
        functools.partial(reduce_kernel, chips, lines),
        out_shape=jax.ShapeDtypeStruct((rows, OBS), f32),
        in_specs=[vmem] * 2,
        out_specs=vmem,
        scratch_shapes=reduce_scratch,
        compiler_params=pltpu.CompilerParams(
            collective_id=1, has_side_effects=True, vmem_limit_bytes=VMEM_BYTES
        ),
        name="reduce",
    )(partial, obs_error.reshape(1, rows))


def solution(mesh):
    placed = (
        P(("groups", "cells"), None, None),
        P(("groups", "cells")),
        P(("groups", "cells")),
        P(("groups", "cells")),
        P(None, ("groups", "cells")),
        P(("groups", "cells")),
    )
    return jax.shard_map(
        local, mesh=mesh, in_specs=placed, out_specs=P(("groups", "cells"), None), check_vma=False
    )
```

```python
import functools

import jax
import jax.numpy as jnp
from jax import lax
from jax.experimental import pallas as pl
from jax.experimental.pallas import tpu as pltpu
from jax.sharding import PartitionSpec as P

WEEKS = 8
OBS = 1024
TILE = 128
SPACE_RANGE = 1.0
TIME_RANGE = 3.0
CHUNKS = 2
SPLIT = 2
VMEM_BYTES = 56 * 1024 * 1024


def place(lines):
    me = lax.axis_index("cells")
    chip = me // 2
    return me, me % 2, chip, chip % lines, chip // lines


def remote(src, dst, send, recv, target):
    return pltpu.make_async_remote_copy(
        src_ref=src,
        dst_ref=dst,
        send_sem=send,
        recv_sem=recv,
        device_id={"cells": target},
        device_id_type=pl.DeviceIdType.MESH,
    )


def signal(sem, target):
    pl.semaphore_signal(
        sem, inc=1, device_id={"cells": target}, device_id_type=pl.DeviceIdType.MESH
    )


def gather_phase(
    chips, lines, own, coords, raw, tiles, home_tiles, covar,
    packet, info, packets, infos, home_pos, pkt_send, pkt_recv, sib_send, sib_recv, hop_send, hop_recv,
    on_places, on_block=None,
):
    depth = chips // lines
    me, core, chip, y, z = place(lines)
    sibling = me + 1 - 2 * core
    slots = own.shape[0]
    part = slots // CHUNKS
    cells = home_pos.shape[1] // 2
    per_dev = cells // TILE

    barrier = pltpu.get_barrier_semaphore()
    for k in range(1, chips):
        signal(barrier, lax.rem(chip + k, chips) * 2 + core)
    signal(barrier, sibling)
    pl.semaphore_wait(barrier, chips)

    packet[...] = jnp.zeros_like(packet)
    for axis in range(2):
        for b in range(per_dev):
            packet[axis * per_dev + b : axis * per_dev + b + 1, :] = coords[
                axis : axis + 1, b * TILE : (b + 1) * TILE
            ]
    info[...] = jnp.zeros_like(info)
    for i, ref in enumerate(raw):
        info[i : i + 1, 0 : ref.shape[1]] = ref[...]

    pkt_copies = []
    for i, (src, dst) in enumerate(((packet, packets), (info, infos))):
        pkt_copies.append(
            remote(src, dst.at[chips], pkt_send.at[i, 0], pkt_recv.at[i, 0], sibling)
        )
        for k in range(1, chips):
            pkt_copies.append(
                remote(src, dst.at[chip], pkt_send.at[i, k], pkt_recv.at[i, k],
                       lax.rem(chip + k, chips) * 2 + core)
            )
    for copy in pkt_copies:
        copy.start()

    def block(q, ch):
        return tiles.at[pl.ds(q * slots + ch * part, part)]

    sends = []

    def send(cond, kind, step, q, ch, target, first):
        source = own.at[pl.ds(ch * part, part)] if first else block(q, ch)
        copy = remote(source, block(q, ch), hop_send.at[kind, step, ch],
                      hop_recv.at[q * CHUNKS + ch], target)
        sends.append((cond, copy))
        if cond is None:
            copy.start()
        else:
            pl.when(cond)(copy.start)

    def arrive(q, ch):
        remote(block(q, ch), block(q, ch), hop_send.at[0, 0, 0],
               hop_recv.at[q * CHUNKS + ch], sibling).wait_recv()

    above = me + 2 * lines
    below = me - 2 * lines
    across = me + 2 - 4 * y
    for ch in range(CHUNKS):
        send(z < depth - 1, 0, 0, chip, ch, above, True)
        send(z > 0, 1, 0, chip, ch, below, True)
        if lines == 2:
            send(None, 2, 0, chip, ch, across, True)
    sib_copy = remote(own, home_tiles.at[pl.ds(core * slots, slots)], sib_send, sib_recv, sibling)
    sib_copy.start()
    tiles[pl.ds(chip * slots, slots)] = own[...]
    home_tiles[pl.ds(core * slots, slots)] = own[...]
    packets[chip] = packet[...]
    infos[chip] = info[...]

    for copy in pkt_copies:
        copy.wait()

    mine = packet[...]
    other = packets[chips]
    is_first = (core == 0).astype(jnp.float32)
    pair = (mine * is_first + other * (1.0 - is_first), other * is_first + mine * (1.0 - is_first))
    for j in range(2):
        columns = jnp.transpose(pair[j])
        for b in range(per_dev):
            rows = pl.ds(j * cells + b * TILE, TILE)
            for axis in range(2):
                col = columns[:, axis * per_dev + b : axis * per_dev + b + 1]
                home_pos[axis, rows, :] = jnp.broadcast_to(col, (TILE, TILE))

    step_rows = 64

    def distances(q):
        for b in range(per_dev):
            east = packets[q, b : b + 1, :]
            north = packets[q, per_dev + b : per_dev + b + 1, :]

            @pl.loop(0, home_pos.shape[1] // step_rows)
            def _(i):
                rows = pl.ds(i * step_rows, step_rows)
                dx = home_pos[0, rows, :] - east
                dy = home_pos[1, rows, :] - north
                covar[q * per_dev + b, rows, :] = jnp.exp(
                    -jnp.sqrt(dx * dx + dy * dy) / SPACE_RANGE
                ).astype(jnp.bfloat16)

    def done(q, ch):
        if on_block is not None:
            on_block(q, ch)

    def from_across(d, ch):
        def low():
            arrive((z - d) * lines + 1 - y, ch)
            done((z - d) * lines + 1 - y, ch)

        def high():
            arrive((z + d) * lines + 1 - y, ch)
            done((z + d) * lines + 1 - y, ch)

        pl.when(z >= d)(low)
        if d > 0:
            pl.when(z + d < depth)(high)

    pl.loop(0, chips // 2)(distances)

    for d in range(1, depth):
        for ch in range(CHUNKS):
            def from_below(d=d, ch=ch):
                arrive((z - d) * lines + y, ch)

            def from_above(d=d, ch=ch):
                arrive((z + d) * lines + y, ch)

            q_low = (z - d) * lines + y
            q_high = (z + d) * lines + y
            pl.when(z >= d)(from_below)
            if d < depth - 1:
                send((z >= d) & (z < depth - 1), 0, d, q_low, ch, above, False)
            if lines == 2:
                send(z >= d, 2, d, q_low, ch, across, False)
            pl.when(z + d < depth)(from_above)
            if d < depth - 1:
                send((z + d < depth) & (z > 0), 1, d, q_high, ch, below, False)
            if lines == 2:
                send(z + d < depth, 3, d, q_high, ch, across, False)
            if d == 1 and ch == 0:
                pl.loop(chips // 2, chips)(distances)
        if d == 1:
            first = jnp.broadcast_to(core == 0, info.shape)
            on_places((
                jnp.where(first, info[...], infos[chips]), jnp.where(first, infos[chips], info[...])
            ))
            for ch in range(CHUNKS):
                done(chip, ch)
        for ch in range(CHUNKS):
            if on_block is not None:
                pl.when(z >= d)(lambda: on_block((z - d) * lines + y, ch))
                pl.when(z + d < depth)(lambda: on_block((z + d) * lines + y, ch))
        if lines == 2:
            for ch in range(CHUNKS):
                from_across(d - 1, ch)
    if lines == 2:
        for ch in range(CHUNKS):
            from_across(depth - 1, ch)
    for cond, copy in sends:
        if cond is None:
            copy.wait_send()
        else:
            pl.when(cond)(copy.wait_send)
    sib_copy.wait()


def gather_kernel(
    chips, lines, own, coords, row_in, col_in, count_in, tiles, home_tiles, covar, meta,
    packet, info, packets, infos, home_pos, pkt_send, pkt_recv, sib_send, sib_recv, hop_send, hop_recv,
):
    def on_places(pair):
        for q in range(chips):
            meta[q] = infos[q]
        for j in range(2):
            meta[chips + j] = pair[j]

    gather_phase(
        chips, lines, own, coords, (row_in, col_in, count_in), tiles, home_tiles, covar,
        packet, info, packets, infos, home_pos, pkt_send, pkt_recv, sib_send, sib_recv, hop_send, hop_recv,
        on_places,
    )


def spread_kernel(chips, meta, tiles, home_tiles, covar, out, acc, weighted):
    slots = tiles.shape[0] // chips
    homes = covar.shape[1]
    cells = homes // 2
    per_dev = cells // TILE
    row_tiles = OBS // TILE

    @pl.loop(0, WEEKS * row_tiles)
    def _(i):
        acc[i] = jnp.zeros((homes, TILE), jnp.float32)

    def place_of(d, s):
        col = meta[d, 1, s]
        return meta[d, 0, s], col // per_dev, col % per_dev

    @pl.loop(0, chips)
    def _(q):
        @pl.loop(0, meta[q, 2, 0])
        def _(s):
            row, week, b = place_of(q, s)
            strip = covar[q * per_dev + b]
            product = lax.dot_general(
                strip, tiles[q * slots + s], (((1,), (1,)), ((), ())),
                preferred_element_type=jnp.float32,
            )
            acc[week * row_tiles + row] += product

    decay = jnp.exp(jnp.float32(-1.0 / TIME_RANGE))
    step_rows = 16
    for r in range(row_tiles):
        @pl.loop(0, homes // step_rows)
        def _(i):
            rows = pl.ds(i * step_rows, step_rows)
            spread = [acc[w * row_tiles + r, rows, :] for w in range(WEEKS)]
            ahead = [spread[0]]
            for w in range(1, WEEKS):
                ahead.append(spread[w] + decay * ahead[-1])
            back = None
            for w in reversed(range(WEEKS)):
                total = ahead[w] if back is None else ahead[w] + back
                weighted[w, rows, r * TILE : (r + 1) * TILE] = total.astype(jnp.bfloat16)
                back = decay * (spread[w] if back is None else spread[w] + back)

    out[...] = jnp.zeros_like(out)
    for j in range(2):
        @pl.loop(0, meta[chips + j, 2, 0])
        def _(s):
            row, week, b = place_of(chips + j, s)
            slab = weighted[week, pl.ds(pl.multiple_of(j * cells + b * TILE, TILE), TILE), :]
            product = jnp.dot(
                home_tiles[j * slots + s], slab, preferred_element_type=jnp.float32
            )
            out[pl.ds(pl.multiple_of(row * TILE, TILE), TILE), :] += product


def reduce_phase(
    chips, lines, obs, out, sib, y_out, y_in, z_out, z_in,
    sib_send, sib_recv, y_send, y_recv, z_send, z_recv, prepare, outgoing, mine,
):
    depth = chips // lines
    me, core, chip, y, z = place(lines)
    sibling = me + 1 - 2 * core
    rows = out.shape[0]
    width = out.shape[1] // SPLIT
    above = me + 2 * lines
    below = me - 2 * lines
    across = me + 2 - 4 * y
    up_ok = z < depth - 1
    down_ok = z > 0
    upper = (z >= depth // 2).astype(jnp.int32)

    def order(j):
        if j == depth - 1:
            return z
        high = depth - 1 - j
        high = high - (high <= z).astype(jnp.int32)
        low = j + (j >= z).astype(jnp.int32)
        return upper * low + (1 - upper) * high

    def sib_copy(h, q):
        return remote(
            outgoing(h, q), sib.at[h, q], sib_send.at[h, q], sib_recv.at[h, q], sibling
        )

    def chip_sum(h, q):
        sib_copy(h, q).wait_recv()
        return mine(h, q) + sib[h, q]

    def y_copy(h, c):
        return remote(y_out.at[h, c], y_in.at[h, c], y_send.at[h, c], y_recv.at[h, c], across)

    def up_copy(h, c):
        return remote(z_out.at[h, c], z_in.at[h, 0, c], z_send.at[h, c], z_recv.at[h, 0, c], above)

    def down_copy(h, c):
        return remote(z_out.at[h, c], z_in.at[h, 1, c], z_send.at[h, c], z_recv.at[h, 1, c], below)

    def y_stage(h):
        for j in range(depth):
            c = order(j)
            y_out[h, c] = chip_sum(h, c * lines + 1 - y).astype(jnp.bfloat16)
            y_copy(h, c).start()

    for h in range(SPLIT):
        prepare(h)
        for line in reversed(range(lines)):
            for j in range(depth):
                sib_copy(h, order(j) * lines + (y + line) % lines).start()
        if lines == 2 and h > 0:
            y_stage(h - 1)
    if lines == 2:
        y_stage(SPLIT - 1)

    def column_sum(h, c):
        total = chip_sum(h, c * lines + y)
        if lines == 2:
            y_copy(h, c).wait_recv()
            total = total + y_in[h, c].astype(jnp.float32)
        return total

    for h in range(SPLIT):
        for j in range(depth - 1):
            c = order(j)
            part = (slice(None), slice(h * width, (h + 1) * width))
            out[part] = column_sum(h, c)

            @pl.when((c > z) & down_ok)
            def _():
                up_copy(h, c).wait_recv()
                out[part] += z_in[h, 0, c].astype(jnp.float32)

            @pl.when((c < z) & up_ok)
            def _():
                down_copy(h, c).wait_recv()
                out[part] += z_in[h, 1, c].astype(jnp.float32)

            z_out[h, c] = out[part].astype(jnp.bfloat16)

            @pl.when(c > z)
            def _():
                up_copy(h, c).start()

            @pl.when(c < z)
            def _():
                down_copy(h, c).start()

    shape = (rows, rows)
    eye = lax.broadcasted_iota(jnp.int32, shape, 0) == lax.broadcasted_iota(jnp.int32, shape, 1)
    errors = jnp.sum(
        jnp.where(eye, jnp.broadcast_to(obs[...], shape), 0.0), axis=1, keepdims=True
    )
    for h in range(SPLIT):
        part = (slice(None), slice(h * width, (h + 1) * width))
        block = (rows, width)
        hit = h * width + lax.broadcasted_iota(jnp.int32, block, 1) == (
            me * rows + lax.broadcasted_iota(jnp.int32, block, 0)
        )
        out[part] = column_sum(h, z) + jnp.where(hit, jnp.broadcast_to(errors, block), 0.0)

        @pl.when(down_ok)
        def _():
            up_copy(h, z).wait_recv()
            out[part] += z_in[h, 0, z].astype(jnp.float32)

        @pl.when(up_ok)
        def _():
            down_copy(h, z).wait_recv()
            out[part] += z_in[h, 1, z].astype(jnp.float32)

    for h in range(SPLIT):
        for q in range(chips):
            sib_copy(h, q).wait_send()
        for c in range(depth):
            if lines == 2:
                y_copy(h, c).wait_send()
            pl.when(c != z)(lambda: up_copy(h, c).wait_send())


def reduce_kernel(chips, lines, partial, obs, out, *scratch):
    depth = chips // lines
    me, core, chip, y, z = place(lines)
    rows = out.shape[0]
    above = me + 2 * lines
    below = me - 2 * lines
    up_ok = z < depth - 1
    down_ok = z > 0
    sibling = me + 1 - 2 * core
    across = me + 2 - 4 * y

    barrier = pltpu.get_barrier_semaphore()
    signal(barrier, sibling)
    if lines == 2:
        signal(barrier, across)
    pl.when(up_ok)(lambda: signal(barrier, above))
    pl.when(down_ok)(lambda: signal(barrier, below))
    pl.semaphore_wait(barrier, lines + up_ok.astype(jnp.int32) + down_ok.astype(jnp.int32))

    width = out.shape[1] // SPLIT

    def slab(h, q, k):
        return partial.at[
            pl.ds(pl.multiple_of((q * 2 + k) * rows, 8), rows), pl.ds(h * width, width)
        ]

    reduce_phase(
        chips, lines, obs, out, *scratch,
        lambda h: None, lambda h, q: slab(h, q, 1 - core), lambda h, q: slab(h, q, core)[...],
    )


def sort_tables(key):
    square = (TILE, TILE)
    of_lane = jnp.broadcast_to(key, square)
    of_row = jnp.transpose(of_lane)
    row = lax.broadcasted_iota(jnp.int32, square, 0)
    lane = lax.broadcasted_iota(jnp.int32, square, 1)

    def count(hits):
        return jnp.sum(jnp.where(hits, 1, 0), axis=0, keepdims=True)

    same_before = (of_row == of_lane) & (row < lane)
    rank = count((of_row < of_lane) | same_before)
    repeat = jnp.where(count(same_before) > 0, 1, 0)
    here = jnp.transpose(jnp.broadcast_to(rank, square)) == lane

    def ordered(values):
        column = jnp.transpose(jnp.broadcast_to(values, square))
        return jnp.sum(jnp.where(here, column, 0), axis=0, keepdims=True)

    perm = ordered(lane[0:1, :])
    held = count(of_row == lane)
    end = count(of_row <= lane) - 1
    return ordered, perm, ordered(repeat), end, held


def fused_kernel(
    chips, lines, own, coords, row_in, col_in, count_in, obs, out,
    tiles, home_tiles, covar, products, runs, weighted, home_runs, sib_out,
    places, whole_tab, share_tab, whole_s, share_s, tab_sem,
    packet, info, packets, infos, home_pos, pkt_send, pkt_recv, sib_send, sib_recv, hop_send, hop_recv,
    sib, y_out, y_in, z_out, z_in, ex_send, ex_recv, y_send, y_recv, z_send, z_recv,
):
    slots = own.shape[0]
    part = slots // CHUNKS
    total = chips * slots
    homes = home_pos.shape[1]
    cells = homes // 2
    per_dev = cells // TILE
    row_tiles = OBS // TILE
    rows = out.shape[0]
    core = lax.axis_index("cells") % 2

    def places_of(values):
        n = len(values) * slots
        row = lax.broadcasted_iota(jnp.int32, (TILE, TILE), 0)
        lane = lax.broadcasted_iota(jnp.int32, (TILE, TILE), 1)
        slot = lane % slots
        picked = []
        for k, at in enumerate((slot, slot, 0)):
            places[k] = jnp.zeros((TILE, TILE), jnp.int32)
            for i, value in enumerate(values):
                places[k, i * slots : (i + 1) * slots, :] = jnp.broadcast_to(
                    value[k : k + 1, :], (slots, TILE)
                )
            known = jnp.transpose(places[k])
            picked.append(jnp.sum(jnp.where(row == at, known, 0), axis=0, keepdims=True))
        row_tile, col_tile, count = picked
        live = (slot[0:1, :] < count) & (lane[0:1, :] < n)
        week = lax.shift_right_logical(col_tile, jnp.full_like(col_tile, per_dev // 2))
        return row_tile, week, col_tile - per_dev * week, live

    def table(row, values):
        whole_tab[row : row + 1, :] = values

    def on_places(pair):
        row_tile, week, cell_block, live = places_of([infos[q] for q in range(chips)])
        key = jnp.where(live, row_tile * WEEKS + week, WEEKS * row_tiles)
        _, perm, keep, end, held = sort_tables(key)
        table(0, perm)
        table(1, jnp.where(held > 0, end, total))
        table(2, cell_block)
        share_tab[0:1, :] = keep.astype(jnp.float32)
        row_tile, week, cell_block, live = places_of(pair)
        key = jnp.where(live, row_tile, row_tiles)
        ordered, perm, keep, end, held = sort_tables(key)
        table(3, perm)
        table(4, jnp.where(held > 0, end, 2 * slots))
        table(5, ordered(week))
        lane = lax.broadcasted_iota(jnp.int32, (1, TILE), 1)
        table(6, ordered(cell_block + jnp.where(lane < slots, 0, per_dev)))
        table(7, jnp.zeros((1, TILE), jnp.int32))
        share_tab[1:2, :] = keep.astype(jnp.float32)
        share_tab[2:8, :] = jnp.zeros((6, TILE), jnp.float32)
        for i, (src, dst) in enumerate(((whole_tab, whole_s), (share_tab, share_s))):
            copy = pltpu.make_async_copy(src, dst, tab_sem.at[i])
            copy.start()
            copy.wait()

    def on_block(q, ch):
        @pl.loop(0, part)
        def _(s):
            t = q * slots + ch * part + s
            products[t] = lax.dot_general(
                covar[q * per_dev + whole_s[2, t]], tiles[t], (((1,), (1,)), ((), ())),
                preferred_element_type=jnp.float32,
            )

    gather_phase(
        chips, lines, own, coords, (row_in, col_in, count_in), tiles, home_tiles, covar,
        packet, info, packets, infos, home_pos, pkt_send, pkt_recv, sib_send, sib_recv, hop_send, hop_recv,
        on_places, on_block,
    )

    decay = jnp.exp(jnp.float32(-1.0 / TIME_RANGE))
    step_rows = runs.shape[1]
    runs[total] = jnp.zeros((step_rows, TILE), jnp.float32)

    steps = TILE // step_rows

    @pl.loop(0, homes // step_rows)
    def _(i):
        strip = pl.ds(pl.multiple_of(i * step_rows, step_rows), step_rows)
        inner = pl.ds(pl.multiple_of((i % steps) * step_rows, step_rows), step_rows)
        running = jnp.zeros((step_rows, TILE), jnp.float32)
        for n in range(total):
            running = running * share_s[0, n] + products[whole_s[0, n], strip, :]
            runs[n] = running
        for r in range(row_tiles):
            spread = [runs[whole_s[1, r * WEEKS + w]] for w in range(WEEKS)]
            ahead = [spread[0]]
            for w in range(1, WEEKS):
                ahead.append(spread[w] + decay * ahead[-1])
            back = None
            for w in reversed(range(WEEKS)):
                value = ahead[w] if back is None else ahead[w] + back
                weighted[w, i // steps, inner, r * TILE : (r + 1) * TILE] = value.astype(jnp.bfloat16)
                back = decay * (spread[w] if back is None else spread[w] + back)

    width = OBS // SPLIT

    def half(h, q, k):
        return home_runs[h, whole_s[4, q], pl.ds(pl.multiple_of(k * rows, 8), rows), :]

    def prepare(h):
        home_runs[h, 2 * slots] = jnp.zeros((TILE, width), jnp.float32)

        @pl.loop(0, 2 * slots, unroll=4)
        def _(n):
            value = jnp.dot(
                home_tiles[whole_s[3, n]],
                weighted[whole_s[5, n], whole_s[6, n], :, pl.ds(h * width, width)],
                preferred_element_type=jnp.float32,
            )
            before = home_runs[h, lax.rem(n + 2 * slots, 2 * slots + 1)]
            home_runs[h, n] = value + before * share_s[1, n]

        for q in range(chips):
            sib_out[h, q] = half(h, q, 1 - core)

    reduce_phase(
        chips, lines, obs, out, sib, y_out, y_in, z_out, z_in,
        ex_send, ex_recv, y_send, y_recv, z_send, z_recv,
        prepare, lambda h, q: sib_out.at[h, q], lambda h, q: half(h, q, core),
    )


def local(footprints, tile_rows, tile_cols, tile_counts, coords, obs_error):
    count = lax.axis_size("cells")
    chips = count // 2
    lines = 2 if chips == 8 else 1
    depth = chips // lines
    slots = footprints.shape[0]
    cells = coords.shape[1]
    per_dev = cells // TILE
    rows = OBS // count
    vmem = pl.BlockSpec(memory_space=pltpu.VMEM)
    smem = pl.BlockSpec(memory_space=pltpu.SMEM)
    dma = pltpu.SemaphoreType.DMA

    places = (
        tile_rows.reshape(1, slots), tile_cols.reshape(1, slots), tile_counts.reshape(1, 1)
    )
    f32, bf16 = jnp.float32, jnp.bfloat16
    gather_scratch = [
        pltpu.VMEM((8, TILE), f32),
        pltpu.VMEM((8, TILE), jnp.int32),
        pltpu.VMEM((chips + 1, 8, TILE), f32),
        pltpu.VMEM((chips + 1, 8, TILE), jnp.int32),
        pltpu.VMEM((2, 2 * cells, TILE), f32),
        dma((2, chips)),
        dma((2, chips)),
        dma,
        dma,
        dma((4, depth, CHUNKS)),
        dma((chips * CHUNKS,)),
    ]
    width = OBS // SPLIT
    reduce_scratch = [
        pltpu.VMEM((SPLIT, chips, rows, width), f32),
        pltpu.VMEM((SPLIT, depth, rows, width), bf16),
        pltpu.VMEM((SPLIT, depth, rows, width), bf16),
        pltpu.VMEM((SPLIT, depth, rows, width), bf16),
        pltpu.VMEM((SPLIT, 2, depth, rows, width), bf16),
        dma((SPLIT, chips)),
        dma((SPLIT, chips)),
        dma((SPLIT, depth)),
        dma((SPLIT, depth)),
        dma((SPLIT, depth)),
        dma((SPLIT, 2, depth)),
    ]
    if chips * slots < TILE and chips * TILE == OBS:
        total = chips * slots
        return pl.pallas_call(
            functools.partial(fused_kernel, chips, lines),
            out_shape=jax.ShapeDtypeStruct((rows, OBS), f32),
            in_specs=[vmem] * 6,
            out_specs=vmem,
            scratch_shapes=[
                pltpu.VMEM((total, TILE, TILE), bf16),
                pltpu.VMEM((2 * slots, TILE, TILE), bf16),
                pltpu.VMEM((chips * per_dev, 2 * cells, TILE), bf16),
                pltpu.VMEM((total, 2 * cells, TILE), f32),
                pltpu.VMEM((total + 1, 32, TILE), f32),
                pltpu.VMEM((WEEKS, 2 * per_dev, TILE, OBS), bf16),
                pltpu.VMEM((SPLIT, 2 * slots + 1, TILE, width), f32),
                pltpu.VMEM((SPLIT, chips, rows, width), f32),
                pltpu.VMEM((3, TILE, TILE), jnp.int32),
                pltpu.VMEM((8, TILE), jnp.int32),
                pltpu.VMEM((8, TILE), f32),
                pltpu.SMEM((8, TILE), jnp.int32),
                pltpu.SMEM((8, TILE), f32),
                dma((2,)),
                *gather_scratch,
                *reduce_scratch,
            ],
            compiler_params=pltpu.CompilerParams(
                collective_id=0, has_side_effects=True, vmem_limit_bytes=VMEM_BYTES
            ),
            name="fused",
        )(footprints, coords, *places, obs_error.reshape(1, rows))

    tiles, home_tiles, covar, meta = pl.pallas_call(
        functools.partial(gather_kernel, chips, lines),
        out_shape=(
            jax.ShapeDtypeStruct((chips * slots, TILE, TILE), bf16),
            jax.ShapeDtypeStruct((2 * slots, TILE, TILE), bf16),
            jax.ShapeDtypeStruct((chips * per_dev, 2 * cells, TILE), bf16),
            jax.ShapeDtypeStruct((chips + 2, 8, TILE), jnp.int32),
        ),
        in_specs=[vmem] * 5,
        out_specs=(vmem,) * 4,
        scratch_shapes=gather_scratch,
        compiler_params=pltpu.CompilerParams(
            collective_id=0, has_side_effects=True, vmem_limit_bytes=VMEM_BYTES
        ),
        name="gather",
    )(footprints, coords, *places)

    partial = pl.pallas_call(
        functools.partial(spread_kernel, chips),
        out_shape=jax.ShapeDtypeStruct((OBS, OBS), jnp.float32),
        in_specs=[smem, vmem, vmem, vmem],
        out_specs=vmem,
        scratch_shapes=[
            pltpu.VMEM((WEEKS * OBS // TILE, 2 * cells, TILE), jnp.float32),
            pltpu.VMEM((WEEKS, 2 * cells, OBS), jnp.bfloat16),
        ],
        compiler_params=pltpu.CompilerParams(vmem_limit_bytes=VMEM_BYTES),
        name="spread",
    )(meta, tiles, home_tiles, covar)

    return pl.pallas_call(
        functools.partial(reduce_kernel, chips, lines),
        out_shape=jax.ShapeDtypeStruct((rows, OBS), f32),
        in_specs=[vmem] * 2,
        out_specs=vmem,
        scratch_shapes=reduce_scratch,
        compiler_params=pltpu.CompilerParams(
            collective_id=1, has_side_effects=True, vmem_limit_bytes=VMEM_BYTES
        ),
        name="reduce",
    )(partial, obs_error.reshape(1, rows))


def solution(mesh):
    placed = (
        P(("groups", "cells"), None, None),
        P(("groups", "cells")),
        P(("groups", "cells")),
        P(("groups", "cells")),
        P(None, ("groups", "cells")),
        P(("groups", "cells")),
    )
    return jax.shard_map(
        local, mesh=mesh, in_specs=placed, out_specs=P(("groups", "cells"), None), check_vma=False
    )
```

```python
import functools

import jax
import jax.numpy as jnp
from jax import lax
from jax.experimental import pallas as pl
from jax.experimental.pallas import tpu as pltpu
from jax.sharding import PartitionSpec as P

WEEKS = 8
OBS = 1024
TILE = 128
SPACE_RANGE = 1.0
TIME_RANGE = 3.0
CHUNKS = 2
SPLIT = 2
VMEM_BYTES = 56 * 1024 * 1024


def place(lines):
    me = lax.axis_index("cells")
    chip = me // 2
    return me, me % 2, chip, chip % lines, chip // lines


def remote(src, dst, send, recv, target):
    return pltpu.make_async_remote_copy(
        src_ref=src,
        dst_ref=dst,
        send_sem=send,
        recv_sem=recv,
        device_id={"cells": target},
        device_id_type=pl.DeviceIdType.MESH,
    )


def signal(sem, target):
    pl.semaphore_signal(
        sem, inc=1, device_id={"cells": target}, device_id_type=pl.DeviceIdType.MESH
    )


def gather_phase(
    chips, lines, own, coords, raw, tiles, home_tiles, covar,
    packet, info, packets, infos, home_pos, pkt_send, pkt_recv, sib_send, sib_recv, hop_send, hop_recv,
    on_places, on_block=None,
):
    depth = chips // lines
    me, core, chip, y, z = place(lines)
    sibling = me + 1 - 2 * core
    slots = own.shape[0]
    part = slots // CHUNKS
    cells = home_pos.shape[1] // 2
    per_dev = cells // TILE

    barrier = pltpu.get_barrier_semaphore()
    for k in range(1, chips):
        signal(barrier, lax.rem(chip + k, chips) * 2 + core)
    signal(barrier, sibling)
    pl.semaphore_wait(barrier, chips)

    packet[...] = jnp.zeros_like(packet)
    for axis in range(2):
        for b in range(per_dev):
            packet[axis * per_dev + b : axis * per_dev + b + 1, :] = coords[
                axis : axis + 1, b * TILE : (b + 1) * TILE
            ]
    info[...] = jnp.zeros_like(info)
    for i, ref in enumerate(raw):
        info[i : i + 1, 0 : ref.shape[1]] = ref[...]

    pkt_copies = []
    for i, (src, dst) in enumerate(((packet, packets), (info, infos))):
        pkt_copies.append(
            remote(src, dst.at[chips], pkt_send.at[i, 0], pkt_recv.at[i, 0], sibling)
        )
        for k in range(1, chips):
            pkt_copies.append(
                remote(src, dst.at[chip], pkt_send.at[i, k], pkt_recv.at[i, k],
                       lax.rem(chip + k, chips) * 2 + core)
            )
    for copy in pkt_copies:
        copy.start()

    def block(q, ch):
        return tiles.at[pl.ds(q * slots + ch * part, part)]

    sends = []

    def send(cond, kind, step, q, ch, target, first):
        source = own.at[pl.ds(ch * part, part)] if first else block(q, ch)
        copy = remote(source, block(q, ch), hop_send.at[kind, step, ch],
                      hop_recv.at[q * CHUNKS + ch], target)
        sends.append((cond, copy))
        if cond is None:
            copy.start()
        else:
            pl.when(cond)(copy.start)

    def arrive(q, ch):
        remote(block(q, ch), block(q, ch), hop_send.at[0, 0, 0],
               hop_recv.at[q * CHUNKS + ch], sibling).wait_recv()

    above = me + 2 * lines
    below = me - 2 * lines
    across = me + 2 - 4 * y
    for ch in range(CHUNKS):
        send(z < depth - 1, 0, 0, chip, ch, above, True)
        send(z > 0, 1, 0, chip, ch, below, True)
        if lines == 2:
            send(None, 2, 0, chip, ch, across, True)
    sib_copy = remote(own, home_tiles.at[pl.ds(core * slots, slots)], sib_send, sib_recv, sibling)
    sib_copy.start()
    tiles[pl.ds(chip * slots, slots)] = own[...]
    home_tiles[pl.ds(core * slots, slots)] = own[...]
    packets[chip] = packet[...]
    infos[chip] = info[...]

    for copy in pkt_copies:
        copy.wait()

    mine = packet[...]
    other = packets[chips]
    is_first = (core == 0).astype(jnp.float32)
    pair = (mine * is_first + other * (1.0 - is_first), other * is_first + mine * (1.0 - is_first))
    for j in range(2):
        columns = jnp.transpose(pair[j])
        for b in range(per_dev):
            rows = pl.ds(j * cells + b * TILE, TILE)
            for axis in range(2):
                col = columns[:, axis * per_dev + b : axis * per_dev + b + 1]
                home_pos[axis, rows, :] = jnp.broadcast_to(col, (TILE, TILE))

    step_rows = 64

    def distances(q):
        for b in range(per_dev):
            east = packets[q, b : b + 1, :]
            north = packets[q, per_dev + b : per_dev + b + 1, :]

            @pl.loop(0, home_pos.shape[1] // step_rows)
            def _(i):
                rows = pl.ds(i * step_rows, step_rows)
                dx = home_pos[0, rows, :] - east
                dy = home_pos[1, rows, :] - north
                covar[q * per_dev + b, rows, :] = jnp.exp(
                    -jnp.sqrt(dx * dx + dy * dy) / SPACE_RANGE
                ).astype(jnp.bfloat16)

    def done(q, ch):
        if on_block is not None:
            on_block(q, ch)

    def from_across(d, ch):
        def low():
            arrive((z - d) * lines + 1 - y, ch)
            done((z - d) * lines + 1 - y, ch)

        def high():
            arrive((z + d) * lines + 1 - y, ch)
            done((z + d) * lines + 1 - y, ch)

        pl.when(z >= d)(low)
        if d > 0:
            pl.when(z + d < depth)(high)

    pl.loop(0, chips // 2)(distances)

    for d in range(1, depth):
        for ch in range(CHUNKS):
            def from_below(d=d, ch=ch):
                arrive((z - d) * lines + y, ch)

            def from_above(d=d, ch=ch):
                arrive((z + d) * lines + y, ch)

            q_low = (z - d) * lines + y
            q_high = (z + d) * lines + y
            pl.when(z >= d)(from_below)
            if d < depth - 1:
                send((z >= d) & (z < depth - 1), 0, d, q_low, ch, above, False)
            if lines == 2:
                send(z >= d, 2, d, q_low, ch, across, False)
            pl.when(z + d < depth)(from_above)
            if d < depth - 1:
                send((z + d < depth) & (z > 0), 1, d, q_high, ch, below, False)
            if lines == 2:
                send(z + d < depth, 3, d, q_high, ch, across, False)
            if d == 1 and ch == 0:
                pl.loop(chips // 2, chips)(distances)
        if d == 1:
            first = jnp.broadcast_to(core == 0, info.shape)
            on_places((
                jnp.where(first, info[...], infos[chips]), jnp.where(first, infos[chips], info[...])
            ))
            for ch in range(CHUNKS):
                done(chip, ch)
        for ch in range(CHUNKS):
            if on_block is not None:
                pl.when(z >= d)(lambda: on_block((z - d) * lines + y, ch))
                pl.when(z + d < depth)(lambda: on_block((z + d) * lines + y, ch))
        if lines == 2:
            for ch in range(CHUNKS):
                from_across(d - 1, ch)
    if lines == 2:
        for ch in range(CHUNKS):
            from_across(depth - 1, ch)
    for cond, copy in sends:
        if cond is None:
            copy.wait_send()
        else:
            pl.when(cond)(copy.wait_send)
    sib_copy.wait()


def gather_kernel(
    chips, lines, own, coords, row_in, col_in, count_in, tiles, home_tiles, covar, meta,
    packet, info, packets, infos, home_pos, pkt_send, pkt_recv, sib_send, sib_recv, hop_send, hop_recv,
):
    def on_places(pair):
        for q in range(chips):
            meta[q] = infos[q]
        for j in range(2):
            meta[chips + j] = pair[j]

    gather_phase(
        chips, lines, own, coords, (row_in, col_in, count_in), tiles, home_tiles, covar,
        packet, info, packets, infos, home_pos, pkt_send, pkt_recv, sib_send, sib_recv, hop_send, hop_recv,
        on_places,
    )


def spread_kernel(chips, meta, tiles, home_tiles, covar, out, acc, weighted):
    slots = tiles.shape[0] // chips
    homes = covar.shape[1]
    cells = homes // 2
    per_dev = cells // TILE
    row_tiles = OBS // TILE

    @pl.loop(0, WEEKS * row_tiles)
    def _(i):
        acc[i] = jnp.zeros((homes, TILE), jnp.float32)

    def place_of(d, s):
        col = meta[d, 1, s]
        return meta[d, 0, s], col // per_dev, col % per_dev

    @pl.loop(0, chips)
    def _(q):
        @pl.loop(0, meta[q, 2, 0])
        def _(s):
            row, week, b = place_of(q, s)
            strip = covar[q * per_dev + b]
            product = lax.dot_general(
                strip, tiles[q * slots + s], (((1,), (1,)), ((), ())),
                preferred_element_type=jnp.float32,
            )
            acc[week * row_tiles + row] += product

    decay = jnp.exp(jnp.float32(-1.0 / TIME_RANGE))
    step_rows = 16
    for r in range(row_tiles):
        @pl.loop(0, homes // step_rows)
        def _(i):
            rows = pl.ds(i * step_rows, step_rows)
            spread = [acc[w * row_tiles + r, rows, :] for w in range(WEEKS)]
            ahead = [spread[0]]
            for w in range(1, WEEKS):
                ahead.append(spread[w] + decay * ahead[-1])
            back = None
            for w in reversed(range(WEEKS)):
                total = ahead[w] if back is None else ahead[w] + back
                weighted[w, rows, r * TILE : (r + 1) * TILE] = total.astype(jnp.bfloat16)
                back = decay * (spread[w] if back is None else spread[w] + back)

    out[...] = jnp.zeros_like(out)
    for j in range(2):
        @pl.loop(0, meta[chips + j, 2, 0])
        def _(s):
            row, week, b = place_of(chips + j, s)
            slab = weighted[week, pl.ds(pl.multiple_of(j * cells + b * TILE, TILE), TILE), :]
            product = jnp.dot(
                home_tiles[j * slots + s], slab, preferred_element_type=jnp.float32
            )
            out[pl.ds(pl.multiple_of(row * TILE, TILE), TILE), :] += product


def reduce_phase(
    chips, lines, obs, out, sib, y_out, y_in, z_out, z_in,
    sib_send, sib_recv, y_send, y_recv, z_send, z_recv, prepare, outgoing, mine,
):
    depth = chips // lines
    me, core, chip, y, z = place(lines)
    sibling = me + 1 - 2 * core
    rows = out.shape[0]
    width = out.shape[1] // SPLIT
    above = me + 2 * lines
    below = me - 2 * lines
    across = me + 2 - 4 * y
    up_ok = z < depth - 1
    down_ok = z > 0
    upper = (z >= depth // 2).astype(jnp.int32)

    def order(j):
        if j == depth - 1:
            return z
        high = depth - 1 - j
        high = high - (high <= z).astype(jnp.int32)
        low = j + (j >= z).astype(jnp.int32)
        return upper * low + (1 - upper) * high

    def sib_copy(h, q):
        return remote(
            outgoing(h, q), sib.at[h, q], sib_send.at[h, q], sib_recv.at[h, q], sibling
        )

    def chip_sum(h, q):
        sib_copy(h, q).wait_recv()
        return mine(h, q) + sib[h, q]

    def y_copy(h, c):
        return remote(y_out.at[h, c], y_in.at[h, c], y_send.at[h, c], y_recv.at[h, c], across)

    def up_copy(h, c):
        return remote(z_out.at[h, c], z_in.at[h, 0, c], z_send.at[h, c], z_recv.at[h, 0, c], above)

    def down_copy(h, c):
        return remote(z_out.at[h, c], z_in.at[h, 1, c], z_send.at[h, c], z_recv.at[h, 1, c], below)

    def y_stage(h):
        for j in range(depth):
            c = order(j)
            y_out[h, c] = chip_sum(h, c * lines + 1 - y).astype(jnp.bfloat16)
            y_copy(h, c).start()

    for h in range(SPLIT):
        prepare(h)
        for line in reversed(range(lines)):
            for j in range(depth):
                sib_copy(h, order(j) * lines + (y + line) % lines).start()
        if lines == 2 and h > 0:
            y_stage(h - 1)
    if lines == 2:
        y_stage(SPLIT - 1)

    def column_sum(h, c):
        total = chip_sum(h, c * lines + y)
        if lines == 2:
            y_copy(h, c).wait_recv()
            total = total + y_in[h, c].astype(jnp.float32)
        return total

    for h in range(SPLIT):
        for j in range(depth - 1):
            c = order(j)
            part = (slice(None), slice(h * width, (h + 1) * width))
            out[part] = column_sum(h, c)

            @pl.when((c > z) & down_ok)
            def _():
                up_copy(h, c).wait_recv()
                out[part] += z_in[h, 0, c].astype(jnp.float32)

            @pl.when((c < z) & up_ok)
            def _():
                down_copy(h, c).wait_recv()
                out[part] += z_in[h, 1, c].astype(jnp.float32)

            z_out[h, c] = out[part].astype(jnp.bfloat16)

            @pl.when(c > z)
            def _():
                up_copy(h, c).start()

            @pl.when(c < z)
            def _():
                down_copy(h, c).start()

    shape = (rows, rows)
    eye = lax.broadcasted_iota(jnp.int32, shape, 0) == lax.broadcasted_iota(jnp.int32, shape, 1)
    errors = jnp.sum(
        jnp.where(eye, jnp.broadcast_to(obs[...], shape), 0.0), axis=1, keepdims=True
    )
    for h in range(SPLIT):
        part = (slice(None), slice(h * width, (h + 1) * width))
        block = (rows, width)
        hit = h * width + lax.broadcasted_iota(jnp.int32, block, 1) == (
            me * rows + lax.broadcasted_iota(jnp.int32, block, 0)
        )
        out[part] = column_sum(h, z) + jnp.where(hit, jnp.broadcast_to(errors, block), 0.0)

        @pl.when(down_ok)
        def _():
            up_copy(h, z).wait_recv()
            out[part] += z_in[h, 0, z].astype(jnp.float32)

        @pl.when(up_ok)
        def _():
            down_copy(h, z).wait_recv()
            out[part] += z_in[h, 1, z].astype(jnp.float32)

    for h in range(SPLIT):
        for q in range(chips):
            sib_copy(h, q).wait_send()
        for c in range(depth):
            if lines == 2:
                y_copy(h, c).wait_send()
            pl.when(c != z)(lambda: up_copy(h, c).wait_send())


def reduce_kernel(chips, lines, partial, obs, out, *scratch):
    depth = chips // lines
    me, core, chip, y, z = place(lines)
    rows = out.shape[0]
    above = me + 2 * lines
    below = me - 2 * lines
    up_ok = z < depth - 1
    down_ok = z > 0
    sibling = me + 1 - 2 * core
    across = me + 2 - 4 * y

    barrier = pltpu.get_barrier_semaphore()
    signal(barrier, sibling)
    if lines == 2:
        signal(barrier, across)
    pl.when(up_ok)(lambda: signal(barrier, above))
    pl.when(down_ok)(lambda: signal(barrier, below))
    pl.semaphore_wait(barrier, lines + up_ok.astype(jnp.int32) + down_ok.astype(jnp.int32))

    width = out.shape[1] // SPLIT

    def slab(h, q, k):
        return partial.at[
            pl.ds(pl.multiple_of((q * 2 + k) * rows, 8), rows), pl.ds(h * width, width)
        ]

    reduce_phase(
        chips, lines, obs, out, *scratch,
        lambda h: None, lambda h, q: slab(h, q, 1 - core), lambda h, q: slab(h, q, core)[...],
    )


def sort_tables(key):
    square = (TILE, TILE)
    of_lane = jnp.broadcast_to(key, square)
    of_row = jnp.transpose(of_lane)
    row = lax.broadcasted_iota(jnp.int32, square, 0)
    lane = lax.broadcasted_iota(jnp.int32, square, 1)

    def count(hits):
        return jnp.sum(jnp.where(hits, 1, 0), axis=0, keepdims=True)

    same_before = (of_row == of_lane) & (row < lane)
    rank = count((of_row < of_lane) | same_before)
    repeat = jnp.where(count(same_before) > 0, 1, 0)
    here = jnp.transpose(jnp.broadcast_to(rank, square)) == lane

    def ordered(values):
        column = jnp.transpose(jnp.broadcast_to(values, square))
        return jnp.sum(jnp.where(here, column, 0), axis=0, keepdims=True)

    perm = ordered(lane[0:1, :])
    held = count(of_row == lane)
    end = count(of_row <= lane) - 1
    return ordered, perm, ordered(repeat), end, held


def fused_kernel(
    chips, lines, own, coords, row_in, col_in, count_in, obs, out,
    tiles, home_tiles, covar, products, runs, weighted, home_runs, sib_out,
    places, whole_tab, share_tab, whole_s, share_s, tab_sem,
    packet, info, packets, infos, home_pos, pkt_send, pkt_recv, sib_send, sib_recv, hop_send, hop_recv,
    sib, y_out, y_in, z_out, z_in, ex_send, ex_recv, y_send, y_recv, z_send, z_recv,
):
    slots = own.shape[0]
    part = slots // CHUNKS
    total = chips * slots
    homes = home_pos.shape[1]
    cells = homes // 2
    per_dev = cells // TILE
    row_tiles = OBS // TILE
    rows = out.shape[0]
    core = lax.axis_index("cells") % 2

    def places_of(values):
        n = len(values) * slots
        row = lax.broadcasted_iota(jnp.int32, (TILE, TILE), 0)
        lane = lax.broadcasted_iota(jnp.int32, (TILE, TILE), 1)
        slot = lane % slots
        picked = []
        for k, at in enumerate((slot, slot, 0)):
            places[k] = jnp.zeros((TILE, TILE), jnp.int32)
            for i, value in enumerate(values):
                places[k, i * slots : (i + 1) * slots, :] = jnp.broadcast_to(
                    value[k : k + 1, :], (slots, TILE)
                )
            known = jnp.transpose(places[k])
            picked.append(jnp.sum(jnp.where(row == at, known, 0), axis=0, keepdims=True))
        row_tile, col_tile, count = picked
        live = (slot[0:1, :] < count) & (lane[0:1, :] < n)
        week = lax.shift_right_logical(col_tile, jnp.full_like(col_tile, per_dev // 2))
        return row_tile, week, col_tile - per_dev * week, live

    def table(row, values):
        whole_tab[row : row + 1, :] = values

    def on_places(pair):
        row_tile, week, cell_block, live = places_of([infos[q] for q in range(chips)])
        key = jnp.where(live, row_tile * WEEKS + week, WEEKS * row_tiles)
        _, perm, keep, end, held = sort_tables(key)
        table(0, perm)
        table(1, jnp.where(held > 0, end, total))
        table(2, cell_block)
        share_tab[0:1, :] = keep.astype(jnp.float32)
        row_tile, week, cell_block, live = places_of(pair)
        key = jnp.where(live, row_tile, row_tiles)
        ordered, perm, keep, end, held = sort_tables(key)
        table(3, perm)
        table(4, jnp.where(held > 0, end, 2 * slots))
        table(5, ordered(week))
        lane = lax.broadcasted_iota(jnp.int32, (1, TILE), 1)
        table(6, ordered(cell_block + jnp.where(lane < slots, 0, per_dev)))
        table(7, jnp.zeros((1, TILE), jnp.int32))
        share_tab[1:2, :] = keep.astype(jnp.float32)
        share_tab[2:8, :] = jnp.zeros((6, TILE), jnp.float32)
        for i, (src, dst) in enumerate(((whole_tab, whole_s), (share_tab, share_s))):
            copy = pltpu.make_async_copy(src, dst, tab_sem.at[i])
            copy.start()
            copy.wait()

    def on_block(q, ch):
        @pl.loop(0, part, unroll=part)
        def _(s):
            t = q * slots + ch * part + s
            products[t] = lax.dot_general(
                covar[q * per_dev + whole_s[2, t]], tiles[t], (((1,), (1,)), ((), ())),
                preferred_element_type=jnp.float32,
            )

    gather_phase(
        chips, lines, own, coords, (row_in, col_in, count_in), tiles, home_tiles, covar,
        packet, info, packets, infos, home_pos, pkt_send, pkt_recv, sib_send, sib_recv, hop_send, hop_recv,
        on_places, on_block,
    )

    decay = jnp.exp(jnp.float32(-1.0 / TIME_RANGE))
    step_rows = runs.shape[1]
    runs[total] = jnp.zeros((step_rows, TILE), jnp.float32)

    steps = TILE // step_rows

    @pl.loop(0, homes // step_rows)
    def _(i):
        strip = pl.ds(pl.multiple_of(i * step_rows, step_rows), step_rows)
        running = jnp.zeros((step_rows, TILE), jnp.float32)
        for n in range(total):
            running = running * share_s[0, n] + products[whole_s[0, n], strip, :]
            runs[n] = running
        for r in range(row_tiles):
            ends = [whole_s[1, r * WEEKS + w] for w in range(WEEKS)]
            for k in range(step_rows // 16):
                spread = [runs[end, k * 16 : (k + 1) * 16, :] for end in ends]
                ahead = [spread[0]]
                for w in range(1, WEEKS):
                    ahead.append(spread[w] + decay * ahead[-1])
                back = None
                lines_at = pl.ds(pl.multiple_of((i % steps) * step_rows + k * 16, 16), 16)
                for w in reversed(range(WEEKS)):
                    value = ahead[w] if back is None else ahead[w] + back
                    weighted[w, i // steps, lines_at, r * TILE : (r + 1) * TILE] = value.astype(
                        jnp.bfloat16
                    )
                    back = decay * (spread[w] if back is None else spread[w] + back)

    width = OBS // SPLIT

    def half(h, q, k):
        return home_runs[h, whole_s[4, q], pl.ds(pl.multiple_of(k * rows, 8), rows), :]

    def prepare(h):
        home_runs[h, 2 * slots] = jnp.zeros((TILE, width), jnp.float32)

        @pl.loop(0, 2 * slots, unroll=2 * slots)
        def _(n):
            value = jnp.dot(
                home_tiles[whole_s[3, n]],
                weighted[whole_s[5, n], whole_s[6, n], :, pl.ds(h * width, width)],
                preferred_element_type=jnp.float32,
            )
            before = home_runs[h, lax.rem(n + 2 * slots, 2 * slots + 1)]
            home_runs[h, n] = value + before * share_s[1, n]

        for q in range(chips):
            sib_out[h, q] = half(h, q, 1 - core)

    reduce_phase(
        chips, lines, obs, out, sib, y_out, y_in, z_out, z_in,
        ex_send, ex_recv, y_send, y_recv, z_send, z_recv,
        prepare, lambda h, q: sib_out.at[h, q], lambda h, q: half(h, q, core),
    )


def local(footprints, tile_rows, tile_cols, tile_counts, coords, obs_error):
    count = lax.axis_size("cells")
    chips = count // 2
    lines = 2 if chips == 8 else 1
    depth = chips // lines
    slots = footprints.shape[0]
    cells = coords.shape[1]
    per_dev = cells // TILE
    rows = OBS // count
    vmem = pl.BlockSpec(memory_space=pltpu.VMEM)
    smem = pl.BlockSpec(memory_space=pltpu.SMEM)
    dma = pltpu.SemaphoreType.DMA

    places = (
        tile_rows.reshape(1, slots), tile_cols.reshape(1, slots), tile_counts.reshape(1, 1)
    )
    f32, bf16 = jnp.float32, jnp.bfloat16
    gather_scratch = [
        pltpu.VMEM((8, TILE), f32),
        pltpu.VMEM((8, TILE), jnp.int32),
        pltpu.VMEM((chips + 1, 8, TILE), f32),
        pltpu.VMEM((chips + 1, 8, TILE), jnp.int32),
        pltpu.VMEM((2, 2 * cells, TILE), f32),
        dma((2, chips)),
        dma((2, chips)),
        dma,
        dma,
        dma((4, depth, CHUNKS)),
        dma((chips * CHUNKS,)),
    ]
    width = OBS // SPLIT
    reduce_scratch = [
        pltpu.VMEM((SPLIT, chips, rows, width), f32),
        pltpu.VMEM((SPLIT, depth, rows, width), bf16),
        pltpu.VMEM((SPLIT, depth, rows, width), bf16),
        pltpu.VMEM((SPLIT, depth, rows, width), bf16),
        pltpu.VMEM((SPLIT, 2, depth, rows, width), bf16),
        dma((SPLIT, chips)),
        dma((SPLIT, chips)),
        dma((SPLIT, depth)),
        dma((SPLIT, depth)),
        dma((SPLIT, depth)),
        dma((SPLIT, 2, depth)),
    ]
    if chips * slots < TILE and chips * TILE == OBS:
        total = chips * slots
        return pl.pallas_call(
            functools.partial(fused_kernel, chips, lines),
            out_shape=jax.ShapeDtypeStruct((rows, OBS), f32),
            in_specs=[vmem] * 6,
            out_specs=vmem,
            scratch_shapes=[
                pltpu.VMEM((total, TILE, TILE), bf16),
                pltpu.VMEM((2 * slots, TILE, TILE), bf16),
                pltpu.VMEM((chips * per_dev, 2 * cells, TILE), bf16),
                pltpu.VMEM((total, 2 * cells, TILE), f32),
                pltpu.VMEM((total + 1, 32, TILE), f32),
                pltpu.VMEM((WEEKS, 2 * per_dev, TILE, OBS), bf16),
                pltpu.VMEM((SPLIT, 2 * slots + 1, TILE, width), f32),
                pltpu.VMEM((SPLIT, chips, rows, width), f32),
                pltpu.VMEM((3, TILE, TILE), jnp.int32),
                pltpu.VMEM((8, TILE), jnp.int32),
                pltpu.VMEM((8, TILE), f32),
                pltpu.SMEM((8, TILE), jnp.int32),
                pltpu.SMEM((8, TILE), f32),
                dma((2,)),
                *gather_scratch,
                *reduce_scratch,
            ],
            compiler_params=pltpu.CompilerParams(
                collective_id=0, has_side_effects=True, vmem_limit_bytes=VMEM_BYTES
            ),
            name="fused",
        )(footprints, coords, *places, obs_error.reshape(1, rows))

    tiles, home_tiles, covar, meta = pl.pallas_call(
        functools.partial(gather_kernel, chips, lines),
        out_shape=(
            jax.ShapeDtypeStruct((chips * slots, TILE, TILE), bf16),
            jax.ShapeDtypeStruct((2 * slots, TILE, TILE), bf16),
            jax.ShapeDtypeStruct((chips * per_dev, 2 * cells, TILE), bf16),
            jax.ShapeDtypeStruct((chips + 2, 8, TILE), jnp.int32),
        ),
        in_specs=[vmem] * 5,
        out_specs=(vmem,) * 4,
        scratch_shapes=gather_scratch,
        compiler_params=pltpu.CompilerParams(
            collective_id=0, has_side_effects=True, vmem_limit_bytes=VMEM_BYTES
        ),
        name="gather",
    )(footprints, coords, *places)

    partial = pl.pallas_call(
        functools.partial(spread_kernel, chips),
        out_shape=jax.ShapeDtypeStruct((OBS, OBS), jnp.float32),
        in_specs=[smem, vmem, vmem, vmem],
        out_specs=vmem,
        scratch_shapes=[
            pltpu.VMEM((WEEKS * OBS // TILE, 2 * cells, TILE), jnp.float32),
            pltpu.VMEM((WEEKS, 2 * cells, OBS), jnp.bfloat16),
        ],
        compiler_params=pltpu.CompilerParams(vmem_limit_bytes=VMEM_BYTES),
        name="spread",
    )(meta, tiles, home_tiles, covar)

    return pl.pallas_call(
        functools.partial(reduce_kernel, chips, lines),
        out_shape=jax.ShapeDtypeStruct((rows, OBS), f32),
        in_specs=[vmem] * 2,
        out_specs=vmem,
        scratch_shapes=reduce_scratch,
        compiler_params=pltpu.CompilerParams(
            collective_id=1, has_side_effects=True, vmem_limit_bytes=VMEM_BYTES
        ),
        name="reduce",
    )(partial, obs_error.reshape(1, rows))


def solution(mesh):
    placed = (
        P(("groups", "cells"), None, None),
        P(("groups", "cells")),
        P(("groups", "cells")),
        P(("groups", "cells")),
        P(None, ("groups", "cells")),
        P(("groups", "cells")),
    )
    return jax.shard_map(
        local, mesh=mesh, in_specs=placed, out_specs=P(("groups", "cells"), None), check_vma=False
    )
```
